512 devices in a mesh: ctx: 64 (over x, z, core), tp: 8 (over y).
Axes of the slice: x: 4, y: 8, z: 8, core: 2. Of those that a mesh axis runs over, the one named last changes fastest.
Arguments:
- tokens: bfloat16 [32768, 2048], P('ctx', 'tp'), may hold values from -2 to 2
- w_query: bfloat16 [2048, 2048], P('ctx', 'tp'), may hold values from -0.125 to 0.125
- w_key: bfloat16 [2048, 2048], P('ctx', 'tp'), may hold values from -0.125 to 0.125
- w_value: bfloat16 [2048, 2048], P('ctx', 'tp'), may hold values from -0.125 to 0.125
- features: float32 [16, 256, 128], P('tp'), may hold values from -4 to 4
- w_out: bfloat16 [2048, 2048], P('tp', 'ctx'), may hold values from -0.125 to 0.125
Outputs:
- mixed: bfloat16 [32768, 2048], P('ctx', 'tp')
The draws below stay inside these ranges and needn't reach their ends.
All inputs are finite; a program needn't handle non-finite values.
Results may differ from the reference program's by a relative error of at most 0.022.
Values may be sent and summed in bfloat16 or wider, within the bound.
A program may use at most 64 MiB of HBM per device.

```python
import jax
import jax.numpy as jnp
from jax import lax

D = 2048
HEADS = 16
DH = 128
MF = 256
TOK_DEV = 512
TOKENS = 32768
HEADS_DEV = 2
N_TP = 8


def draw_tokens(key, part):
    key = jax.random.fold_in(key, 11)
    value_key = jax.random.fold_in(key, 0)
    values = jnp.clip(0.5 * jax.random.normal(value_key, (TOKENS, D), jnp.float32), -2.0, 2.0)
    return values.astype(jnp.bfloat16)


def level_of(stream_key, shape, pieces, least, high):
    def one(position, blocks):
        draws = jax.random.uniform(jax.random.fold_in(jax.random.fold_in(stream_key, 6), position), (blocks,), jnp.float32, least / len(pieces), high / len(pieces))
        return jnp.repeat(jnp.exp(draws), shape[position] // blocks).reshape((-1,) + (1,) * (len(shape) - position - 1))

    loudness = one(*pieces[0])
    for cut in pieces[1:]:
        loudness = loudness * one(*cut)
    return loudness


def noise(stream_key, shape, deviation, reach, shards=(), held_as=jnp.bfloat16):
    result = deviation * jax.random.normal(stream_key, shape, jnp.float32)
    if shards:
        result = result * level_of(stream_key, shape, shards, -0.22, 0.18)
    return jnp.clip(result, -reach, reach).astype(held_as)


def setup_inputs(seed: int = 0) -> dict:
    seeds = jax.random.split(jax.random.key(seed), 7)
    tokens = draw_tokens(jax.random.fold_in(seeds[6], 71), 0)
    w_query = noise(seeds[1], (D, HEADS * DH), D ** -0.5, 0.125, ((0, 64), (1, 8)))
    w_key = noise(seeds[2], (D, HEADS * DH), D ** -0.5, 0.125, ((0, 64), (1, 8)))
    w_value = noise(seeds[3], (D, HEADS * DH), D ** -0.5, 0.125, ((0, 64), (1, 8)))
    features = noise(seeds[4], (HEADS, MF, DH), 1.0, 4.0, ((0, 8),), jnp.float32)
    w_out = noise(seeds[5], (HEADS * DH, D), (HEADS * DH) ** -0.5, 0.125, ((0, 8), (1, 64)))
    return dict(tokens=tokens, w_query=w_query, w_key=w_key, w_value=w_value, features=features, w_out=w_out)


def positive(projected, features):
    count = projected.shape[0]
    scaled_logits = projected.reshape(count, HEADS, DH) * (DH ** -0.25)
    feature_logits = jnp.einsum("rxy,xzy->xrz", scaled_logits, features, precision=lax.Precision.HIGHEST)
    half_square = 0.5 * jnp.sum(scaled_logits * scaled_logits, axis=-1)
    return jnp.exp(feature_logits - jnp.transpose(half_square)[:, :, None])


def reference(tokens, w_query, w_key, w_value, features, w_out):
    block = min(TOK_DEV, 512)
    steps_total = TOKENS // block
    stacked = tokens.reshape(steps_total, block, D)
    causal = jnp.tril(jnp.ones((block, block), dtype=bool))
    out_groups = w_out.astype(jnp.float32).reshape(N_TP, HEADS_DEV * DH, D)
    highest_precision = lax.Precision.HIGHEST

    def advance(carry, rows):
        running_state, normal = carry
        query = jnp.dot(rows, w_query, preferred_element_type=jnp.float32)
        key = jnp.dot(rows, w_key, preferred_element_type=jnp.float32)
        value = jnp.dot(rows, w_value, preferred_element_type=jnp.float32)
        query_feature_map = positive(query, features)
        key_feature_map = positive(key, features)
        per_head_value = jnp.transpose(value.reshape(block, HEADS, DH), (1, 0, 2))
        scores = jnp.einsum("hqm,hkm->hqk", query_feature_map, key_feature_map, precision=highest_precision)
        scores = jnp.where(causal[None], scores, jnp.float32(0.0))
        numerator_sum = jnp.einsum("hqk,hkd->hqd", scores, per_head_value, precision=highest_precision)
        numerator_sum = numerator_sum + jnp.einsum("twl,tlb->twb", query_feature_map, running_state, precision=highest_precision)
        denom = jnp.sum(scores, axis=-1) + jnp.einsum("hqm,hm->hq", query_feature_map, normal, precision=highest_precision)
        attn = (numerator_sum / denom[:, :, None]).astype(jnp.bfloat16)
        attn = jnp.transpose(attn, (1, 0, 2)).reshape(block, N_TP, HEADS_DEV * DH)
        partial_value = jnp.einsum("tgc,gcd->gtd", attn.astype(jnp.float32), out_groups, precision=highest_precision)
        partial_value = lax.optimization_barrier(partial_value.astype(jnp.bfloat16))
        mixed_rows = jnp.sum(partial_value.astype(jnp.float32), axis=0).astype(jnp.bfloat16)
        running_state = running_state + jnp.einsum("sfj,sft->sjt", key_feature_map, per_head_value, precision=highest_precision)
        normal = normal + jnp.sum(key_feature_map, axis=1)
        return (running_state, normal), mixed_rows

    start = (jnp.zeros((HEADS, MF, DH), jnp.float32), jnp.zeros((HEADS, MF), jnp.float32))
    final, outputs = lax.scan(advance, start, stacked)
    return outputs.reshape(TOKENS, D)
```

```python
import jax
import jax.numpy as jnp
from jax import lax
from jax.experimental import pallas as pl
from jax.experimental.pallas import tpu as pltpu
from jax.sharding import PartitionSpec as P

NX, NZ, NC, NY = 4, 8, 2, 8
GROUP = NZ * NC
TOK = 512
HALF = 256
WIDTH = 256
DH = 128
MF = 256
SHARD = 32
SLICE = 16
SENDS = 128
BF = jnp.bfloat16
F32 = jnp.float32
NT = (((1,), (1,)), ((), ()))
TN = (((0,), (0,)), ((), ()))


def kernel(
    tok_ref, wq_ref, wk_ref, wv_ref, feat_ref, wo_ref, out_ref,
    tok, w, kv, q, vaug, phik, phiq, fcat, nd, ssend, precv, excl, tot, psend, pfx, attn,
    rs_send, rs_recv,
    ssem, tok_sem, z_sem, x_sem, sib_sem, a_sem, b_sem, c_sem, rs_sem,
):
    ctx = lax.axis_index("ctx")
    y = lax.axis_index("tp")
    c = lax.rem(ctx, NC)
    z = lax.rem(lax.div(ctx, NC), NZ)
    x = lax.div(ctx, GROUP)
    me16 = lax.rem(ctx, GROUP)

    def at(xx, zz, cc):
        return {"ctx": (xx * NZ + zz) * NC + cc, "tp": y}

    def at_y(yy):
        return {"ctx": ctx, "tp": yy}

    def turn(v, by, n):
        return lax.rem(v + (by % n), n)

    def peer16(d):
        return turn(me16, d, GROUP)

    def dev16(p):
        return {"ctx": x * GROUP + p, "tp": y}

    ups = [at_y(turn(y, 1, NY)), at_y(turn(y, -1, NY))]
    sides = [at(turn(x, 1, NX), z, c), at(turn(x, -1, NX), z, c)]
    sib = at(x, z, 1 - c)

    barrier = pltpu.get_barrier_semaphore()
    greeted = (
        [dev16(peer16(d)) for d in range(1, GROUP)]
        + [at(turn(x, d, NX), z, c) for d in range(1, NX)]
        + ups
    )
    for p in greeted:
        pl.semaphore_signal(barrier, inc=1, device_id=p, device_id_type=pl.DeviceIdType.MESH)

    tok[y] = tok_ref[...]
    w[x, z, c, 0] = wk_ref[...]
    w[x, z, c, 1] = wv_ref[...]
    w[x, z, c, 2] = wq_ref[...]
    rows = lax.broadcasted_iota(jnp.int32, (SHARD, SHARD), 0)
    cols = lax.broadcasted_iota(jnp.int32, (SHARD, SHARD), 1)
    eye = (rows == cols).astype(F32).astype(BF)
    w[x, z, c, 3] = lax.dot_general(eye, wo_ref[...], NT, preferred_element_type=F32).astype(BF)

    pl.semaphore_wait(barrier, len(greeted))

    sends = []

    def send(src, dst, rsem, dev):
        copy = pltpu.make_async_remote_copy(
            src_ref=src, dst_ref=dst, send_sem=ssem.at[len(sends)], recv_sem=rsem,
            device_id=dev, device_id_type=pl.DeviceIdType.MESH,
        )
        copy.start()
        sends.append(copy)

    def recv(dst, rsem):
        pltpu.make_async_copy(dst, dst, rsem).wait()

    def tok_owner(d, step):
        return turn(y, -step if d == 0 else step, NY)

    def tok_part(owner, r):
        return tok.at[owner, pl.ds(r * HALF, HALF)]

    def tok_send(d, step, r):
        part = tok_part(tok_owner(d, step), r)
        send(part, part, tok_sem.at[d, step, r], ups[d])

    def tok_recv(d, step, r):
        recv(tok_part(tok_owner(d, step + 1), r), tok_sem.at[d, step, r])

    def w_part(xx, zs, cc, part):
        return w.at[xx, zs, cc, pl.ds(2 * part, 2)]

    def z_send(part):
        own = w_part(x, z, c, part)
        for d in (4, 3, 5, 2, 6, 1, 7):
            send(own, own, z_sem.at[part, z], at(x, turn(z, d, NZ), c))

    def z_recv(part):
        for d in (1, 7, 2, 6, 3, 5, 4):
            zz = turn(z, d, NZ)
            recv(w_part(x, zz, c, part), z_sem.at[part, zz])

    every = pl.ds(0, NZ)
    halves = (pl.ds(0, NZ // 2), pl.ds(NZ // 2, NZ // 2))

    def x_start(part):
        block = w_part(x, every, c, part)
        for d in range(2):
            send(block, block, x_sem.at[part, d], sides[d])

    def sib_send(part, i, xx, zs):
        block = w_part(xx, zs, c, part)
        send(block, block, sib_sem.at[part, i], sib)

    def x_near(part):
        for d in range(2):
            xx = turn(x, -1 if d == 0 else 1, NX)
            recv(w_part(xx, every, c, part), x_sem.at[part, d])
            half = w_part(xx, halves[d], c, part)
            send(half, half, x_sem.at[part, 2 + d], sides[d])
            sib_send(part, 1 + d, xx, every)

    def x_far(part):
        xx = turn(x, 2, NX)
        for d in range(2):
            recv(w_part(xx, halves[d], c, part), x_sem.at[part, 2 + d])
            sib_send(part, 3 + d, xx, halves[d])

    def sib_recv(part):
        o = 1 - c
        blocks = [
            (x, every), (turn(x, -1, NX), every), (turn(x, 1, NX), every),
            (turn(x, 2, NX), halves[0]), (turn(x, 2, NX), halves[1]),
        ]
        for i, (xx, zs) in enumerate(blocks):
            recv(w_part(xx, zs, o, part), sib_sem.at[part, i])

    for r in range(2):
        for d in range(2):
            tok_send(d, 0, r)
    z_send(0)
    z_send(1)

    for h in range(2):
        f = feat_ref[h]
        hi = f.astype(BF)
        lo = (f - hi.astype(F32)).astype(BF)
        fcat[h] = jnp.concatenate([hi, hi, lo], axis=1)

    z_recv(0)
    x_start(0)
    sib_send(0, 0, x, every)

    for r in range(2):
        for d in range(2):
            tok_recv(d, 0, r)
            tok_send(d, 1, r)

    z_recv(1)
    sib_send(1, 0, x, every)
    x_near(0)
    x_start(1)

    for r in range(2):
        for d in range(2):
            tok_recv(d, 1, r)
            tok_send(d, 2, r)

    x_far(0)
    x_near(1)

    tok_recv(0, 2, 0)
    tok_send(0, 3, 0)
    tok_recv(1, 2, 1)
    tok_send(1, 3, 1)

    sib_recv(0)

    def w_rows(s, k):
        return w[lax.div(s, 2), pl.ds(lax.rem(s, 2) * 4, 4), :, k].reshape(WIDTH, WIDTH)

    def kv_term(s, r):
        t = tok[s, pl.ds(r * HALF, HALF)]
        k = jnp.dot(t, w_rows(s, 0), preferred_element_type=F32)
        v = jnp.dot(t, w_rows(s, 1), preferred_element_type=F32)
        return k, v

    def kv_add(s):
        for r in range(2):
            k, v = kv_term(s, r)
            kv[0, pl.ds(r * HALF, HALF)] += k
            kv[1, pl.ds(r * HALF, HALF)] += v

    kv[...] = jnp.zeros_like(kv)

    @pl.loop(0, 5)
    def _(i):
        kv_add(lax.rem(y + i + (NY - 2), NY))

    x_far(1)

    tok_recv(0, 2, 1)
    tok_recv(1, 2, 0)

    @pl.loop(0, 2)
    def _(i):
        kv_add(lax.rem(y + 3 + 2 * i, NY))

    tok_recv(0, 3, 0)
    tok_recv(1, 3, 1)
    kv_add(turn(y, 4, NY))

    def positive(p, h):
        s = p * (DH ** -0.25)
        half_square = 0.5 * jnp.sum(s * s, axis=-1, keepdims=True)
        hi = s.astype(BF)
        lo = (s - hi.astype(F32)).astype(BF)
        logits = lax.dot_general(
            jnp.concatenate([hi, lo, hi], axis=1), fcat[h], NT, preferred_element_type=F32
        )
        return jnp.exp(logits - half_square).astype(BF)

    lane = lax.broadcasted_iota(jnp.int32, (MF, DH), 1)
    sums = []
    for h in range(2):
        head = pl.ds(h * DH, DH)
        vaug[h, :, pl.ds(0, DH)] = kv[1, :, head].astype(BF)
        vaug[h, :, pl.ds(DH, DH)] = jnp.ones((TOK, DH), BF)
        phik[h] = positive(kv[0, :, head], h)
        s = lax.dot_general(phik[h], vaug[h], TN, preferred_element_type=F32)
        ssend[:, head] = s[:, :DH].astype(BF)
        sums.append(s[:, DH:])
    ssend[:, pl.ds(2 * DH, DH)] = jnp.where(lane < DH // 2, sums[0], sums[1]).astype(BF)

    for d in range(1, GROUP):
        p = peer16(d)
        send(
            ssend.at[pl.ds(pl.multiple_of(p * SLICE, SLICE), SLICE)],
            precv.at[me16], a_sem.at[me16], dev16(p),
        )
    precv[me16] = ssend[pl.ds(pl.multiple_of(me16 * SLICE, SLICE), SLICE)]

    sib_recv(1)

    @pl.loop(0, NY)
    def _(s):
        for r in range(2):
            t = tok[s, pl.ds(r * HALF, HALF)]
            term = jnp.dot(t, w_rows(s, 2), preferred_element_type=F32)
            rows_r = pl.ds(r * HALF, HALF)

            @pl.when(s == 0)
            def _():
                q[rows_r] = term

            @pl.when(s > 0)
            def _():
                q[rows_r] += term

    for d in range(1, GROUP):
        p = peer16(d)
        recv(precv.at[p], a_sem.at[p])
    run = jnp.zeros((SLICE, 3 * DH), F32)
    for i in range(GROUP):
        excl[i] = run
        run = run + precv[i].astype(F32)
    tot[x] = run
    for d in range(1, NX):
        send(tot.at[x], tot.at[x], b_sem.at[x], at(turn(x, d, NX), z, c))

    def local(h):
        head = pl.ds(h * DH, DH)
        phiq[h] = positive(q[:, head], h)
        for r in range(2):
            rows_r = pl.ds(r * HALF, HALF)
            upto = (r + 1) * HALF
            sc = lax.dot_general(
                phiq[h, rows_r], phik[h, pl.ds(0, upto)], NT, preferred_element_type=F32
            )
            row = lax.broadcasted_iota(jnp.int32, (HALF, upto), 0) + r * HALF
            col = lax.broadcasted_iota(jnp.int32, (HALF, upto), 1)
            sc = jnp.where(col <= row, sc, 0.0).astype(BF)
            nd[h, rows_r] = jnp.dot(sc, vaug[h, pl.ds(0, upto)], preferred_element_type=F32)

    local(0)

    for d in range(1, NX):
        xx = turn(x, d, NX)
        recv(tot.at[xx], b_sem.at[xx])
    base = jnp.zeros((SLICE, 3 * DH), F32)
    for i in range(NX):
        base = base + jnp.where(i < x, tot[i], 0.0)
    for i in range(GROUP):
        psend[i] = (excl[i] + base).astype(BF)
    for d in range(1, GROUP):
        p = peer16(d)
        send(psend.at[p], pfx.at[me16], c_sem.at[me16], dev16(p))
    pfx[me16] = psend[me16]

    local(1)

    for d in range(1, GROUP):
        p = peer16(d)
        recv(pfx.at[p], c_sem.at[p])

    prefix = pfx[...].reshape(MF, 3 * DH)
    pick_r = lax.broadcasted_iota(jnp.int32, (DH, 2 * DH), 0)
    pick_c = lax.broadcasted_iota(jnp.int32, (DH, 2 * DH), 1)
    pick = (pick_r == jnp.where(pick_c < DH, 0, DH // 2)).astype(F32).astype(BF)
    spread = jnp.dot(prefix[:, 2 * DH :], pick, preferred_element_type=F32).astype(BF)
    for h in range(2):
        state = jnp.concatenate(
            [prefix[:, h * DH : (h + 1) * DH], spread[:, h * DH : (h + 1) * DH]], axis=1
        )
        full = nd[h] + jnp.dot(phiq[h], state, preferred_element_type=F32)
        attn[:, pl.ds(h * DH, DH)] = (full[:, :DH] / full[:, DH:]).astype(BF)

    def share(dest, r):
        return lax.dot_general(
            attn[pl.ds(r * HALF, HALF)], w_rows(dest, 3), NT, preferred_element_type=F32
        )

    def rs_item(d, step, r, first):
        dest = turn(y, (4 - step) if d == 0 else (step - 4), NY)
        value = share(dest, r)
        if not first:
            recv(rs_recv.at[d, step - 1, r], rs_sem.at[d, step - 1, r])
            value = value + rs_recv[d, step - 1, r].astype(F32)
        rs_send[d, step, r] = value.astype(BF)
        send(rs_send.at[d, step, r], rs_recv.at[d, step, r], rs_sem.at[d, step, r], ups[d])

    for d in range(2):
        rs_item(d, 0, d, True)
    for step in range(1, 4):
        for k in range(2):
            for d in range(2):
                rs_item(d, step, (1 - d) if k == 0 else d, step == 1 and k == 0)
    for r in range(2):
        value = share(y, r)
        for d in range(2):
            recv(rs_recv.at[d, 3, r], rs_sem.at[d, 3, r])
            value = value + rs_recv[d, 3, r].astype(F32)
        out_ref[pl.ds(r * HALF, HALF)] = value.astype(BF)

    for copy in sends:
        copy.wait_send()


def body(tokens, w_query, w_key, w_value, features, w_out):
    vmem = pl.BlockSpec(memory_space=pltpu.VMEM)
    dma = pltpu.SemaphoreType.DMA
    return pl.pallas_call(
        kernel,
        out_shape=jax.ShapeDtypeStruct((TOK, WIDTH), BF),
        in_specs=[vmem] * 6,
        out_specs=vmem,
        scratch_shapes=[
            pltpu.VMEM((NY, TOK, WIDTH), BF),
            pltpu.VMEM((NX, NZ, NC, 4, SHARD, WIDTH), BF),
            pltpu.VMEM((2, TOK, WIDTH), F32),
            pltpu.VMEM((TOK, WIDTH), F32),
            pltpu.VMEM((2, TOK, 2 * DH), BF),
            pltpu.VMEM((2, TOK, MF), BF),
            pltpu.VMEM((2, TOK, MF), BF),
            pltpu.VMEM((2, MF, 3 * DH), BF),
            pltpu.VMEM((2, TOK, 2 * DH), F32),
            pltpu.VMEM((MF, 3 * DH), BF),
            pltpu.VMEM((GROUP, SLICE, 3 * DH), BF),
            pltpu.VMEM((GROUP, SLICE, 3 * DH), F32),
            pltpu.VMEM((NX, SLICE, 3 * DH), F32),
            pltpu.VMEM((GROUP, SLICE, 3 * DH), BF),
            pltpu.VMEM((GROUP, SLICE, 3 * DH), BF),
            pltpu.VMEM((TOK, 2 * DH), BF),
            pltpu.VMEM((2, 4, 2, HALF, WIDTH), BF),
            pltpu.VMEM((2, 4, 2, HALF, WIDTH), BF),
            dma((SENDS,)),
            dma((2, 4, 2)),
            dma((2, NZ)),
            dma((2, 4)),
            dma((2, 5)),
            dma((GROUP,)),
            dma((NX,)),
            dma((GROUP,)),
            dma((2, 4, 2)),
        ],
        compiler_params=pltpu.CompilerParams(
            collective_id=0, has_side_effects=True, vmem_limit_bytes=48 * 1024 * 1024
        ),
    )(tokens, w_query, w_key, w_value, features, w_out)


def solution(mesh):
    return jax.shard_map(
        body,
        mesh=mesh,
        in_specs=(
            P("ctx", "tp"),
            P("ctx", "tp"),
            P("ctx", "tp"),
            P("ctx", "tp"),
            P("tp", None, None),
            P("tp", "ctx"),
        ),
        out_specs=P("ctx", "tp"),
        check_vma=False,
    )
```

```python
import jax
import jax.numpy as jnp
from jax import lax
from jax.experimental import pallas as pl
from jax.experimental.pallas import tpu as pltpu
from jax.sharding import PartitionSpec as P

NX, NZ, NC, NY = 4, 8, 2, 8
GROUP = NZ * NC
TOK = 512
HALF = 256
WIDTH = 256
DH = 128
MF = 256
SHARD = 32
SLICE = 16
SENDS = 128
BF = jnp.bfloat16
F32 = jnp.float32
NT = (((1,), (1,)), ((), ()))
TN = (((0,), (0,)), ((), ()))


def kernel(
    tok_ref, wq_ref, wk_ref, wv_ref, feat_ref, wo_ref, out_ref,
    tok, w, kv, q, vaug, phik, phiq, feat, fcat, nd, ssend, srecv, tsend, arecv, excl, tot,
    psend, pfx, fsend, frecv, own, attn, rs_send, rs_recv,
    loc_sem, ssem, tok_sem, z_sem, x_sem, sib_sem, a_sem, b_sem, c_sem, j_sem, rs_sem,
):
    ctx = lax.axis_index("ctx")
    y = lax.axis_index("tp")
    c = lax.rem(ctx, NC)
    z = lax.rem(lax.div(ctx, NC), NZ)
    x = lax.div(ctx, GROUP)

    def at(xx, zz, cc):
        return {"ctx": (xx * NZ + zz) * NC + cc, "tp": y}

    def at_y(yy):
        return {"ctx": ctx, "tp": yy}

    def turn(v, by, n):
        return lax.rem(v + (by % n), n)

    ups = [at_y(turn(y, 1, NY)), at_y(turn(y, -1, NY))]
    sides = [at(turn(x, 1, NX), z, c), at(turn(x, -1, NX), z, c)]
    sib = at(x, z, 1 - c)

    barrier = pltpu.get_barrier_semaphore()
    greeted = (
        ups
        + [at(x, turn(z, d, NZ), c) for d in (4, 3, 5, 2, 6, 1, 7)]
        + [at(turn(x, d, NX), z, c) for d in (2, 1, 3)]
        + [sib]
    )
    for p in greeted:
        pl.semaphore_signal(barrier, inc=1, device_id=p, device_id_type=pl.DeviceIdType.MESH)

    loads = [
        pltpu.make_async_copy(src, dst, loc_sem.at[i])
        for i, (src, dst) in enumerate([
            (tok_ref, tok.at[y]),
            (wk_ref, w.at[x, z, c, 0]),
            (wv_ref, w.at[x, z, c, 1]),
            (wq_ref, w.at[x, z, c, 2]),
            (wo_ref, w.at[x, z, c, 3]),
            (feat_ref, feat),
        ])
    ]
    for copy in loads:
        copy.start()
    for copy in loads:
        copy.wait()

    for h in range(2):
        f = feat[h]
        hi = f.astype(BF)
        lo = (f - hi.astype(F32)).astype(BF)
        fcat[h] = jnp.concatenate([hi, hi, lo], axis=1)

    pl.semaphore_wait(barrier, len(greeted))

    sends = []

    def send(src, dst, rsem, dev):
        copy = pltpu.make_async_remote_copy(
            src_ref=src, dst_ref=dst, send_sem=ssem.at[len(sends)], recv_sem=rsem,
            device_id=dev, device_id_type=pl.DeviceIdType.MESH,
        )
        copy.start()
        sends.append(copy)

    def recv(dst, rsem):
        pltpu.make_async_copy(dst, dst, rsem).wait()

    def tok_owner(d, step):
        return turn(y, -step if d == 0 else step, NY)

    def tok_part(owner, r):
        return tok.at[owner, pl.ds(r * HALF, HALF)]

    def tok_send(d, step, r):
        part = tok_part(tok_owner(d, step), r)
        send(part, part, tok_sem.at[d, step, r], ups[d])

    def tok_recv(d, step, r):
        recv(tok_part(tok_owner(d, step + 1), r), tok_sem.at[d, step, r])

    spans = (pl.ds(0, 2), pl.ds(2, 1), pl.ds(3, 1))

    def w_part(xx, zs, cc, part):
        return w.at[xx, zs, cc, spans[part]]

    def z_send(part):
        mine = w_part(x, z, c, part)
        for d in (4, 3, 5, 2, 6, 1, 7):
            send(mine, mine, z_sem.at[part, z], at(x, turn(z, d, NZ), c))

    def z_recv(part):
        for d in (1, 7, 2, 6, 3, 5, 4):
            zz = turn(z, d, NZ)
            recv(w_part(x, zz, c, part), z_sem.at[part, zz])

    every = pl.ds(0, NZ)
    halves = (pl.ds(0, NZ // 2), pl.ds(NZ // 2, NZ // 2))

    def sib_send(part, i, xx, zs):
        block = w_part(xx, zs, c, part)
        send(block, block, sib_sem.at[part, i], sib)

    def x_start(part):
        for i in range(2):
            for d in range(2):
                half = w_part(x, halves[d if i == 0 else 1 - d], c, part)
                send(half, half, x_sem.at[part, 2 * d + i], sides[d])
        sib_send(part, 0, x, every)

    def x_near(part, i):
        for d in range(2):
            xx = turn(x, -1 if d == 0 else 1, NX)
            zs = halves[d if i == 0 else 1 - d]
            half = w_part(xx, zs, c, part)
            recv(half, x_sem.at[part, 2 * d + i])
            if i == 0:
                send(half, half, x_sem.at[part, 4 + d], sides[d])
            sib_send(part, 1 + 2 * d + i, xx, zs)

    def x_far(part):
        xx = turn(x, 2, NX)
        for d in range(2):
            recv(w_part(xx, halves[d], c, part), x_sem.at[part, 4 + d])
            sib_send(part, 5 + d, xx, halves[d])

    def sib_recv(part):
        o = 1 - c
        recv(w_part(x, every, o, part), sib_sem.at[part, 0])
        for d in range(2):
            for i in range(2):
                xx = turn(x, -1 if d == 0 else 1, NX)
                recv(w_part(xx, halves[d if i == 0 else 1 - d], o, part), sib_sem.at[part, 1 + 2 * d + i])
            recv(w_part(turn(x, 2, NX), halves[d], o, part), sib_sem.at[part, 5 + d])

    for r in range(2):
        for d in range(2):
            tok_send(d, 0, r)
    z_send(0)

    def tok_pass(step, r):
        for d in range(2):
            tok_recv(d, step, r)
            tok_send(d, step + 1, r)

    tok_pass(0, 0)
    tok_pass(0, 1)
    z_recv(0)
    x_start(0)
    z_send(1)
    z_send(2)
    tok_pass(1, 0)
    tok_pass(1, 1)
    x_near(0, 0)
    tok_recv(0, 2, 0)
    tok_send(0, 3, 0)
    x_near(0, 1)
    z_recv(1)
    x_start(1)
    tok_recv(1, 2, 1)
    tok_send(1, 3, 1)
    x_far(0)
    z_recv(2)
    sib_recv(0)

    def w_rows(s, k):
        return w[lax.div(s, 2), pl.ds(lax.rem(s, 2) * 4, 4), :, k].reshape(WIDTH, WIDTH)

    def kv_term(s, r):
        t = tok[s, pl.ds(r * HALF, HALF)]
        k = jnp.dot(t, w_rows(s, 0), preferred_element_type=F32)
        v = jnp.dot(t, w_rows(s, 1), preferred_element_type=F32)
        return k, v

    def kv_add(s):
        for r in range(2):
            k, v = kv_term(s, r)
            kv[0, pl.ds(r * HALF, HALF)] += k
            kv[1, pl.ds(r * HALF, HALF)] += v

    kv[...] = jnp.zeros_like(kv)

    @pl.loop(0, 5)
    def _(i):
        kv_add(lax.rem(y + i + (NY - 2), NY))

    x_near(1, 0)

    tok_recv(0, 2, 1)
    tok_recv(1, 2, 0)

    @pl.loop(0, 2)
    def _(i):
        kv_add(lax.rem(y + 3 + 2 * i, NY))

    tok_recv(0, 3, 0)
    tok_recv(1, 3, 1)
    kv_add(turn(y, 4, NY))

    def positive(p, h):
        s = p * (DH ** -0.25)
        half_square = 0.5 * jnp.sum(s * s, axis=-1, keepdims=True)
        hi = s.astype(BF)
        lo = (s - hi.astype(F32)).astype(BF)
        logits = lax.dot_general(
            jnp.concatenate([hi, lo, hi], axis=1), fcat[h], NT, preferred_element_type=F32
        )
        return jnp.exp(logits - half_square).astype(BF)

    def key_sums(h):
        head = pl.ds(pl.multiple_of(h * DH, DH), DH)
        vaug[h, :, pl.ds(0, DH)] = kv[1, :, head].astype(BF)
        vaug[h, :, pl.ds(DH, DH)] = jnp.ones((TOK, DH), BF)
        phik[h] = positive(kv[0, :, head], h)
        return lax.dot_general(phik[h], vaug[h], TN, preferred_element_type=F32)

    ssend[...] = key_sums(1 - c).astype(BF)
    send(ssend, srecv, j_sem.at[0], sib)
    own[...] = key_sums(c).astype(BF).astype(F32)
    recv(srecv, j_sem.at[0])
    chip = own[...] + srecv[...].astype(F32)
    lane = lax.broadcasted_iota(jnp.int32, (NZ, SLICE, DH), 2)
    norm = chip[:, DH:].reshape(NZ, 2, SLICE, DH)
    tsend[:, pl.ds(0, 2 * SLICE)] = chip[:, :DH].reshape(NZ, 2 * SLICE, DH).astype(BF)
    tsend[:, pl.ds(2 * SLICE, SLICE)] = jnp.where(lane < DH // 2, norm[:, 0], norm[:, 1]).astype(BF)

    for d in (4, 3, 5, 2, 6, 1, 7):
        zz = turn(z, d, NZ)
        send(tsend.at[zz], arecv.at[z], a_sem.at[z], at(x, zz, c))
    arecv[z] = tsend[z]

    x_near(1, 1)
    x_start(2)
    x_far(1)
    sib_recv(1)

    @pl.loop(0, NY)
    def _(s):
        for r in range(2):
            t = tok[s, pl.ds(r * HALF, HALF)]
            term = jnp.dot(t, w_rows(s, 2), preferred_element_type=F32)
            rows_r = pl.ds(r * HALF, HALF)

            @pl.when(s == 0)
            def _():
                q[rows_r] = term

            @pl.when(s > 0)
            def _():
                q[rows_r] += term

    for h in range(2):
        phiq[h] = positive(q[:, pl.ds(h * DH, DH)], h)

    for d in (1, 7, 2, 6, 3, 5, 4):
        zz = turn(z, d, NZ)
        recv(arecv.at[zz], a_sem.at[zz])
    run = jnp.zeros((3 * SLICE, DH), F32)
    for i in range(NZ):
        excl[i] = run
        run = run + arecv[i].astype(F32)
    tot[x] = run.astype(BF)
    for d in (2, 1, 3):
        send(tot.at[x], tot.at[x], b_sem.at[x], at(turn(x, d, NX), z, c))

    def local(h):
        for r in range(2):
            rows_r = pl.ds(r * HALF, HALF)
            upto = (r + 1) * HALF
            sc = lax.dot_general(
                phiq[h, rows_r], phik[h, pl.ds(0, upto)], NT, preferred_element_type=F32
            )
            row = lax.broadcasted_iota(jnp.int32, (HALF, upto), 0) + r * HALF
            col = lax.broadcasted_iota(jnp.int32, (HALF, upto), 1)
            sc = jnp.where(col <= row, sc, 0.0).astype(BF)
            nd[h, rows_r] = jnp.dot(sc, vaug[h, pl.ds(0, upto)], preferred_element_type=F32)

    x_near(2, 0)
    local(0)

    for d in range(1, NX):
        xx = turn(x, d, NX)
        recv(tot.at[xx], b_sem.at[xx])
    base = jnp.zeros((3 * SLICE, DH), F32)
    for i in range(NX):
        base = base + jnp.where(i < x, tot[i].astype(F32), 0.0)
    for i in range(NZ):
        psend[i] = (excl[i] + base).astype(BF)
    for d in (4, 3, 5, 2, 6, 1, 7):
        zz = turn(z, d, NZ)
        send(psend.at[zz], pfx.at[z], c_sem.at[z], at(x, zz, c))
    pfx[z] = psend[z]

    x_near(2, 1)
    local(1)
    x_far(2)
    sib_recv(2)

    for d in (1, 7, 2, 6, 3, 5, 4):
        zz = turn(z, d, NZ)
        recv(pfx.at[zz], c_sem.at[zz])

    pick_r = lax.broadcasted_iota(jnp.int32, (DH, 2 * DH), 0)
    pick_c = lax.broadcasted_iota(jnp.int32, (DH, 2 * DH), 1)
    pick = (pick_r == jnp.where(pick_c < DH, 0, DH // 2)).astype(F32).astype(BF)
    spread = jnp.dot(
        pfx[:, pl.ds(2 * SLICE, SLICE)].reshape(NZ * SLICE, DH), pick, preferred_element_type=F32
    ).reshape(NZ, SLICE, 2 * DH)
    norm = jnp.stack([spread[:, :, :DH], spread[:, :, DH:]], axis=1).reshape(MF, DH)
    before = jnp.concatenate(
        [pfx[:, pl.ds(0, 2 * SLICE)].reshape(MF, DH).astype(F32), norm], axis=1
    )
    fsend[...] = (before + jnp.where(c == 0, own[...], 0.0)).astype(BF)
    send(fsend, frecv, j_sem.at[1], sib)
    state = (before + jnp.where(c == 0, 0.0, srecv[...].astype(F32))).astype(BF)

    def finish(h, state):
        full = nd[h] + jnp.dot(phiq[h], state, preferred_element_type=F32)
        head = pl.ds(pl.multiple_of(h * DH, DH), DH)
        attn[:, head] = (full[:, :DH] / full[:, DH:]).astype(BF)

    finish(c, state)
    recv(frecv, j_sem.at[1])
    finish(1 - c, frecv[...])

    def share(dest, r):
        return lax.dot_general(
            attn[pl.ds(r * HALF, HALF)], w_rows(dest, 3), NT, preferred_element_type=F32
        )

    def rs_item(d, step, r, first):
        dest = turn(y, (4 - step) if d == 0 else (step - 4), NY)
        value = share(dest, r)
        if not first:
            recv(rs_recv.at[d, step - 1, r], rs_sem.at[d, step - 1, r])
            value = value + rs_recv[d, step - 1, r].astype(F32)
        rs_send[d, step, r] = value.astype(BF)
        send(rs_send.at[d, step, r], rs_recv.at[d, step, r], rs_sem.at[d, step, r], ups[d])

    for d in range(2):
        rs_item(d, 0, d, True)
    for step in range(1, 4):
        for k in range(2):
            for d in range(2):
                rs_item(d, step, (1 - d) if k == 0 else d, step == 1 and k == 0)
    for r in range(2):
        value = share(y, r)
        for d in range(2):
            recv(rs_recv.at[d, 3, r], rs_sem.at[d, 3, r])
            value = value + rs_recv[d, 3, r].astype(F32)
        out_ref[pl.ds(r * HALF, HALF)] = value.astype(BF)

    for copy in sends:
        copy.wait_send()


def body(tokens, w_query, w_key, w_value, features, w_out):
    hbm = pl.BlockSpec(memory_space=pl.ANY)
    dma = pltpu.SemaphoreType.DMA
    return pl.pallas_call(
        kernel,
        out_shape=jax.ShapeDtypeStruct((TOK, WIDTH), BF),
        in_specs=[hbm] * 6,
        out_specs=pl.BlockSpec(memory_space=pltpu.VMEM),
        scratch_shapes=[
            pltpu.VMEM((NY, TOK, WIDTH), BF),
            pltpu.VMEM((NX, NZ, NC, 4, SHARD, WIDTH), BF),
            pltpu.VMEM((2, TOK, WIDTH), F32),
            pltpu.VMEM((TOK, WIDTH), F32),
            pltpu.VMEM((2, TOK, 2 * DH), BF),
            pltpu.VMEM((2, TOK, MF), BF),
            pltpu.VMEM((2, TOK, MF), BF),
            pltpu.VMEM((2, MF, DH), F32),
            pltpu.VMEM((2, MF, 3 * DH), BF),
            pltpu.VMEM((2, TOK, 2 * DH), F32),
            pltpu.VMEM((MF, 2 * DH), BF),
            pltpu.VMEM((MF, 2 * DH), BF),
            pltpu.VMEM((NZ, 3 * SLICE, DH), BF),
            pltpu.VMEM((NZ, 3 * SLICE, DH), BF),
            pltpu.VMEM((NZ, 3 * SLICE, DH), F32),
            pltpu.VMEM((NX, 3 * SLICE, DH), BF),
            pltpu.VMEM((NZ, 3 * SLICE, DH), BF),
            pltpu.VMEM((NZ, 3 * SLICE, DH), BF),
            pltpu.VMEM((MF, 2 * DH), BF),
            pltpu.VMEM((MF, 2 * DH), BF),
            pltpu.VMEM((MF, 2 * DH), F32),
            pltpu.VMEM((TOK, 2 * DH), BF),
            pltpu.VMEM((2, 4, 2, HALF, WIDTH), BF),
            pltpu.VMEM((2, 4, 2, HALF, WIDTH), BF),
            dma((6,)),
            dma((SENDS,)),
            dma((2, 4, 2)),
            dma((3, NZ)),
            dma((3, 6)),
            dma((3, 7)),
            dma((NZ,)),
            dma((NX,)),
            dma((NZ,)),
            dma((2,)),
            dma((2, 4, 2)),
        ],
        compiler_params=pltpu.CompilerParams(
            collective_id=0, has_side_effects=True, vmem_limit_bytes=60 * 1024 * 1024
        ),
    )(tokens, w_query, w_key, w_value, features, w_out.T)


def solution(mesh):
    return jax.shard_map(
        body,
        mesh=mesh,
        in_specs=(
            P("ctx", "tp"),
            P("ctx", "tp"),
            P("ctx", "tp"),
            P("ctx", "tp"),
            P("tp", None, None),
            P("tp", "ctx"),
        ),
        out_specs=P("ctx", "tp"),
        check_vma=False,
    )
```

```python
import jax
import jax.numpy as jnp
from jax import lax
from jax.experimental import pallas as pl
from jax.experimental.pallas import tpu as pltpu
from jax.sharding import PartitionSpec as P

NX, NZ, NC, NY = 4, 8, 2, 8
GROUP = NZ * NC
TOK = 512
HALF = 256
PIECES = 4
PIECE = 128
WIDTH = 256
DH = 128
MF = 256
SHARD = 32
SLICE = 16
SENDS = 192
BF = jnp.bfloat16
F32 = jnp.float32
NT = (((1,), (1,)), ((), ()))
TN = (((0,), (0,)), ((), ()))


def kernel(
    tok_ref, wq_ref, wk_ref, wv_ref, feat_ref, wo_ref, out_ref,
    tok, w, kv, q, vaug, phik, phiq, feat, fcat, nd, ssend, srecv, tsend, arecv, excl, tot,
    psend, pfx, fsend, frecv, own, attn, rs_send, rs_recv,
    loc_sem, ssem, tok_sem, z_sem, x_sem, sib_sem, a_sem, b_sem, c_sem, j_sem, rs_sem,
):
    ctx = lax.axis_index("ctx")
    y = lax.axis_index("tp")
    c = lax.rem(ctx, NC)
    z = lax.rem(lax.div(ctx, NC), NZ)
    x = lax.div(ctx, GROUP)

    def at(xx, zz, cc):
        return {"ctx": (xx * NZ + zz) * NC + cc, "tp": y}

    def at_y(yy):
        return {"ctx": ctx, "tp": yy}

    def turn(v, by, n):
        return lax.rem(v + (by % n), n)

    ups = [at_y(turn(y, 1, NY)), at_y(turn(y, -1, NY))]
    sides = [at(turn(x, 1, NX), z, c), at(turn(x, -1, NX), z, c)]
    sib = at(x, z, 1 - c)

    barrier = pltpu.get_barrier_semaphore()
    greeted = (
        ups
        + [at(x, turn(z, d, NZ), c) for d in (4, 3, 5, 2, 6, 1, 7)]
        + [at(turn(x, d, NX), z, c) for d in (2, 1, 3)]
        + [sib]
    )
    for p in greeted:
        pl.semaphore_signal(barrier, inc=1, device_id=p, device_id_type=pl.DeviceIdType.MESH)

    loads = [
        pltpu.make_async_copy(src, dst, loc_sem.at[i])
        for i, (src, dst) in enumerate([
            (tok_ref, tok.at[y]),
            (wk_ref, w.at[x, z, c, 0]),
            (wv_ref, w.at[x, z, c, 1]),
            (wq_ref, w.at[x, z, c, 2]),
            (wo_ref, w.at[x, z, c, 3]),
            (feat_ref, feat),
        ])
    ]
    for copy in loads:
        copy.start()
    pl.semaphore_wait(barrier, len(greeted))

    sends = []

    def send(src, dst, rsem, dev):
        copy = pltpu.make_async_remote_copy(
            src_ref=src, dst_ref=dst, send_sem=ssem.at[len(sends)], recv_sem=rsem,
            device_id=dev, device_id_type=pl.DeviceIdType.MESH,
        )
        copy.start()
        sends.append(copy)

    def recv(dst, rsem):
        pltpu.make_async_copy(dst, dst, rsem).wait()

    def tok_owner(d, step):
        return turn(y, -step if d == 0 else step, NY)

    def tok_part(owner, r):
        return tok.at[owner, pl.ds(r * PIECE, PIECE)]

    def tok_send(d, step, r):
        part = tok_part(tok_owner(d, step), r)
        src = tok_ref.at[pl.ds(r * PIECE, PIECE)] if step == 0 else part
        send(src, part, tok_sem.at[d, step, r], ups[d])

    def tok_recv(d, step, r):
        recv(tok_part(tok_owner(d, step + 1), r), tok_sem.at[d, step, r])

    spans = (pl.ds(0, 2), pl.ds(2, 1), pl.ds(3, 1))

    def w_part(xx, zs, cc, part):
        return w.at[xx, zs, cc, spans[part]]

    def z_send(part):
        mine = w_part(x, z, c, part)
        for d in (4, 3, 5, 2, 6, 1, 7):
            send(mine, mine, z_sem.at[part, z], at(x, turn(z, d, NZ), c))

    def z_recv(part):
        for d in (1, 7, 2, 6, 3, 5, 4):
            zz = turn(z, d, NZ)
            recv(w_part(x, zz, c, part), z_sem.at[part, zz])

    every = pl.ds(0, NZ)
    halves = (pl.ds(0, NZ // 2), pl.ds(NZ // 2, NZ // 2))

    def sib_send(part, i, xx, zs):
        block = w_part(xx, zs, c, part)
        send(block, block, sib_sem.at[part, i], sib)

    def x_start(part):
        for i in range(2):
            for d in range(2):
                half = w_part(x, halves[d if i == 0 else 1 - d], c, part)
                send(half, half, x_sem.at[part, 2 * d + i], sides[d])
        sib_send(part, 0, x, every)

    def x_near(part, i):
        for d in range(2):
            xx = turn(x, -1 if d == 0 else 1, NX)
            zs = halves[d if i == 0 else 1 - d]
            half = w_part(xx, zs, c, part)
            recv(half, x_sem.at[part, 2 * d + i])
            if i == 0:
                send(half, half, x_sem.at[part, 4 + d], sides[d])
            sib_send(part, 1 + 2 * d + i, xx, zs)

    def x_far(part):
        xx = turn(x, 2, NX)
        for d in range(2):
            recv(w_part(xx, halves[d], c, part), x_sem.at[part, 4 + d])
            sib_send(part, 5 + d, xx, halves[d])

    def sib_recv(part):
        o = 1 - c
        recv(w_part(x, every, o, part), sib_sem.at[part, 0])
        for d in range(2):
            for i in range(2):
                xx = turn(x, -1 if d == 0 else 1, NX)
                recv(w_part(xx, halves[d if i == 0 else 1 - d], o, part), sib_sem.at[part, 1 + 2 * d + i])
            recv(w_part(turn(x, 2, NX), halves[d], o, part), sib_sem.at[part, 5 + d])

    for r in range(PIECES):
        for d in range(2):
            tok_send(d, 0, r)
    for copy in loads:
        copy.wait()
    z_send(0)

    for h in range(2):
        f = feat[h]
        hi = f.astype(BF)
        lo = (f - hi.astype(F32)).astype(BF)
        fcat[h] = jnp.concatenate([hi, hi, lo], axis=1)

    def tok_pass(step, r):
        for d in range(2):
            tok_recv(d, step, r)
            tok_send(d, step + 1, r)

    for r in range(PIECES):
        tok_pass(0, r)
    z_recv(0)
    x_start(0)
    z_send(1)
    z_send(2)
    for r in range(PIECES):
        tok_pass(1, r)
    x_near(0, 0)
    for r in range(2):
        tok_recv(0, 2, r)
        tok_send(0, 3, r)
    x_near(0, 1)
    z_recv(1)
    x_start(1)
    for r in range(2, 4):
        tok_recv(1, 2, r)
        tok_send(1, 3, r)
    x_far(0)
    z_recv(2)
    sib_recv(0)

    def w_rows(s, k):
        return w[lax.div(s, 2), pl.ds(lax.rem(s, 2) * 4, 4), :, k].reshape(WIDTH, WIDTH)

    def kv_term(s, r):
        t = tok[s, pl.ds(r * HALF, HALF)]
        k = jnp.dot(t, w_rows(s, 0), preferred_element_type=F32)
        v = jnp.dot(t, w_rows(s, 1), preferred_element_type=F32)
        return k, v

    def kv_add(s):
        for r in range(2):
            k, v = kv_term(s, r)
            kv[0, pl.ds(r * HALF, HALF)] += k
            kv[1, pl.ds(r * HALF, HALF)] += v

    kv[...] = jnp.zeros_like(kv)

    @pl.loop(0, 5)
    def _(i):
        kv_add(lax.rem(y + i + (NY - 2), NY))

    x_near(1, 0)

    for r in range(2):
        tok_recv(0, 2, 2 + r)
        tok_recv(1, 2, r)

    @pl.loop(0, 2)
    def _(i):
        kv_add(lax.rem(y + 3 + 2 * i, NY))

    for r in range(2):
        tok_recv(0, 3, r)
        tok_recv(1, 3, 2 + r)
    kv_add(turn(y, 4, NY))

    def positive(p, h):
        s = p * (DH ** -0.25)
        half_square = 0.5 * jnp.sum(s * s, axis=-1, keepdims=True)
        hi = s.astype(BF)
        lo = (s - hi.astype(F32)).astype(BF)
        logits = lax.dot_general(
            jnp.concatenate([hi, lo, hi], axis=1), fcat[h], NT, preferred_element_type=F32
        )
        return jnp.exp(logits - half_square).astype(BF)

    def key_sums(h):
        head = pl.ds(pl.multiple_of(h * DH, DH), DH)
        vaug[h, :, pl.ds(0, DH)] = kv[1, :, head].astype(BF)
        vaug[h, :, pl.ds(DH, DH)] = jnp.ones((TOK, DH), BF)
        phik[h] = positive(kv[0, :, head], h)
        return lax.dot_general(phik[h], vaug[h], TN, preferred_element_type=F32)

    ssend[...] = key_sums(1 - c).astype(BF)
    send(ssend, srecv, j_sem.at[0], sib)
    own[...] = key_sums(c).astype(BF).astype(F32)
    recv(srecv, j_sem.at[0])
    chip = own[...] + srecv[...].astype(F32)
    lane = lax.broadcasted_iota(jnp.int32, (NZ, SLICE, DH), 2)
    norm = chip[:, DH:].reshape(NZ, 2, SLICE, DH)
    tsend[:, pl.ds(0, 2 * SLICE)] = chip[:, :DH].reshape(NZ, 2 * SLICE, DH).astype(BF)
    tsend[:, pl.ds(2 * SLICE, SLICE)] = jnp.where(lane < DH // 2, norm[:, 0], norm[:, 1]).astype(BF)

    for d in (4, 3, 5, 2, 6, 1, 7):
        zz = turn(z, d, NZ)
        send(tsend.at[zz], arecv.at[z], a_sem.at[z], at(x, zz, c))
    arecv[z] = tsend[z]

    x_near(1, 1)
    x_start(2)
    x_far(1)
    sib_recv(1)

    @pl.loop(0, NY)
    def _(s):
        for r in range(2):
            t = tok[s, pl.ds(r * HALF, HALF)]
            term = jnp.dot(t, w_rows(s, 2), preferred_element_type=F32)
            rows_r = pl.ds(r * HALF, HALF)

            @pl.when(s == 0)
            def _():
                q[rows_r] = term

            @pl.when(s > 0)
            def _():
                q[rows_r] += term

    for d in (1, 7, 2, 6, 3, 5, 4):
        zz = turn(z, d, NZ)
        recv(arecv.at[zz], a_sem.at[zz])
    run = jnp.zeros((3 * SLICE, DH), F32)
    for i in range(NZ):
        excl[i] = run
        run = run + arecv[i].astype(F32)
    tot[x] = run.astype(BF)
    for d in (2, 1, 3):
        send(tot.at[x], tot.at[x], b_sem.at[x], at(turn(x, d, NX), z, c))

    def local(h):
        for r in range(2):
            rows_r = pl.ds(r * HALF, HALF)
            upto = (r + 1) * HALF
            sc = lax.dot_general(
                phiq[h, rows_r], phik[h, pl.ds(0, upto)], NT, preferred_element_type=F32
            )
            row = lax.broadcasted_iota(jnp.int32, (HALF, upto), 0) + r * HALF
            col = lax.broadcasted_iota(jnp.int32, (HALF, upto), 1)
            sc = jnp.where(col <= row, sc, 0.0).astype(BF)
            nd[h, rows_r] = jnp.dot(sc, vaug[h, pl.ds(0, upto)], preferred_element_type=F32)

    x_near(2, 0)
    for h in range(2):
        phiq[h] = positive(q[:, pl.ds(h * DH, DH)], h)
    local(0)

    for d in range(1, NX):
        xx = turn(x, d, NX)
        recv(tot.at[xx], b_sem.at[xx])
    base = jnp.zeros((3 * SLICE, DH), F32)
    for i in range(NX):
        base = base + jnp.where(i < x, tot[i].astype(F32), 0.0)
    for i in range(NZ):
        psend[i] = (excl[i] + base).astype(BF)
    for d in (4, 3, 5, 2, 6, 1, 7):
        zz = turn(z, d, NZ)
        send(psend.at[zz], pfx.at[z], c_sem.at[z], at(x, zz, c))
    pfx[z] = psend[z]

    x_near(2, 1)
    local(1)
    x_far(2)
    sib_recv(2)

    for d in (1, 7, 2, 6, 3, 5, 4):
        zz = turn(z, d, NZ)
        recv(pfx.at[zz], c_sem.at[zz])

    pick_r = lax.broadcasted_iota(jnp.int32, (DH, 2 * DH), 0)
    pick_c = lax.broadcasted_iota(jnp.int32, (DH, 2 * DH), 1)
    pick = (pick_r == jnp.where(pick_c < DH, 0, DH // 2)).astype(F32).astype(BF)
    spread = jnp.dot(
        pfx[:, pl.ds(2 * SLICE, SLICE)].reshape(NZ * SLICE, DH), pick, preferred_element_type=F32
    ).reshape(NZ, SLICE, 2 * DH)
    norm = jnp.stack([spread[:, :, :DH], spread[:, :, DH:]], axis=1).reshape(MF, DH)
    before = jnp.concatenate(
        [pfx[:, pl.ds(0, 2 * SLICE)].reshape(MF, DH).astype(F32), norm], axis=1
    )
    fsend[...] = (before + jnp.where(c == 0, own[...], 0.0)).astype(BF)
    send(fsend, frecv, j_sem.at[1], sib)
    state = (before + jnp.where(c == 0, 0.0, srecv[...].astype(F32))).astype(BF)

    def finish(h, state, r):
        rows_r = pl.ds(r * HALF, HALF)
        full = nd[h, rows_r] + jnp.dot(phiq[h, rows_r], state, preferred_element_type=F32)
        head = pl.ds(pl.multiple_of(h * DH, DH), DH)
        attn[rows_r, head] = (full[:, :DH] / full[:, DH:]).astype(BF)

    def share(dest, r):
        return lax.dot_general(
            attn[pl.ds(r * PIECE, PIECE)], w_rows(dest, 3), NT, preferred_element_type=F32
        )

    def rs_item(d, step, r, first):
        dest = turn(y, (4 - step) if d == 0 else (step - 4), NY)
        value = share(dest, r)
        if not first:
            recv(rs_recv.at[d, step - 1, r], rs_sem.at[d, step - 1, r])
            value = value + rs_recv[d, step - 1, r].astype(F32)
        rs_send[d, step, r] = value.astype(BF)
        send(rs_send.at[d, step, r], rs_recv.at[d, step, r], rs_sem.at[d, step, r], ups[d])

    finish(c, state, 0)
    finish(c, state, 1)
    recv(frecv, j_sem.at[1])
    finish(1 - c, frecv[...], 0)
    for r in range(2):
        rs_item(0, 0, r, True)
    finish(1 - c, frecv[...], 1)
    for r in range(2):
        rs_item(1, 0, 2 + r, True)
    for step in range(1, 4):
        for k in range(4):
            for d in range(2):
                rs_item(d, step, (k + 2 * (1 - d)) % 4, step == 1 and k < 2)
    for r in range(PIECES):
        value = share(y, r)
        for d in range(2):
            recv(rs_recv.at[d, 3, r], rs_sem.at[d, 3, r])
            value = value + rs_recv[d, 3, r].astype(F32)
        out_ref[pl.ds(r * PIECE, PIECE)] = value.astype(BF)

    for copy in sends:
        copy.wait_send()


def body(tokens, w_query, w_key, w_value, features, w_out):
    hbm = pl.BlockSpec(memory_space=pl.ANY)
    dma = pltpu.SemaphoreType.DMA
    return pl.pallas_call(
        kernel,
        out_shape=jax.ShapeDtypeStruct((TOK, WIDTH), BF),
        in_specs=[hbm] * 6,
        out_specs=pl.BlockSpec(memory_space=pltpu.VMEM),
        scratch_shapes=[
            pltpu.VMEM((NY, TOK, WIDTH), BF),
            pltpu.VMEM((NX, NZ, NC, 4, SHARD, WIDTH), BF),
            pltpu.VMEM((2, TOK, WIDTH), F32),
            pltpu.VMEM((TOK, WIDTH), F32),
            pltpu.VMEM((2, TOK, 2 * DH), BF),
            pltpu.VMEM((2, TOK, MF), BF),
            pltpu.VMEM((2, TOK, MF), BF),
            pltpu.VMEM((2, MF, DH), F32),
            pltpu.VMEM((2, MF, 3 * DH), BF),
            pltpu.VMEM((2, TOK, 2 * DH), F32),
            pltpu.VMEM((MF, 2 * DH), BF),
            pltpu.VMEM((MF, 2 * DH), BF),
            pltpu.VMEM((NZ, 3 * SLICE, DH), BF),
            pltpu.VMEM((NZ, 3 * SLICE, DH), BF),
            pltpu.VMEM((NZ, 3 * SLICE, DH), F32),
            pltpu.VMEM((NX, 3 * SLICE, DH), BF),
            pltpu.VMEM((NZ, 3 * SLICE, DH), BF),
            pltpu.VMEM((NZ, 3 * SLICE, DH), BF),
            pltpu.VMEM((MF, 2 * DH), BF),
            pltpu.VMEM((MF, 2 * DH), BF),
            pltpu.VMEM((MF, 2 * DH), F32),
            pltpu.VMEM((TOK, 2 * DH), BF),
            pltpu.VMEM((2, 4, PIECES, PIECE, WIDTH), BF),
            pltpu.VMEM((2, 4, PIECES, PIECE, WIDTH), BF),
            dma((6,)),
            dma((SENDS,)),
            dma((2, 4, PIECES)),
            dma((3, NZ)),
            dma((3, 6)),
            dma((3, 7)),
            dma((NZ,)),
            dma((NX,)),
            dma((NZ,)),
            dma((2,)),
            dma((2, 4, PIECES)),
        ],
        compiler_params=pltpu.CompilerParams(
            collective_id=0, has_side_effects=True, vmem_limit_bytes=56 * 1024 * 1024
        ),
    )(tokens, w_query, w_key, w_value, features, w_out.T)


def solution(mesh):
    return jax.shard_map(
        body,
        mesh=mesh,
        in_specs=(
            P("ctx", "tp"),
            P("ctx", "tp"),
            P("ctx", "tp"),
            P("ctx", "tp"),
            P("tp", None, None),
            P("tp", "ctx"),
        ),
        out_specs=P("ctx", "tp"),
        check_vma=False,
    )
```

```python
import jax
import jax.numpy as jnp
from jax import lax
from jax.experimental import pallas as pl
from jax.experimental.pallas import tpu as pltpu
from jax.sharding import PartitionSpec as P

NX, NZ, NC, NY = 4, 8, 2, 8
GROUP = NZ * NC
TOK = 512
HALF = 256
PIECES = 4
PIECE = 128
WIDTH = 256
DH = 128
MF = 256
SHARD = 32
SLICE = 16
SROWS = DH + SLICE
SENDS = 192
BF = jnp.bfloat16
F32 = jnp.float32
NT = (((1,), (1,)), ((), ()))
TN = (((0,), (0,)), ((), ()))


def kernel(
    tok_ref, wq_ref, wk_ref, wv_ref, feat_ref, wo_ref, out_ref,
    tok, w, kv, q, vaug, phik, phiq, feat, fcat, nd, sacc, ssend, srecv, tsend, arecv, nsend, nrecv,
    excl, tot, ntot, psend, pfx, npre, fsend, frecv, own, attn, rs_send, rs_recv,
    loc_sem, ssem, tok_sem, z_sem, x_sem, sib_sem, a_sem, an_sem, b_sem, bn_sem, c_sem, j_sem, rs_sem,
):
    ctx = lax.axis_index("ctx")
    y = lax.axis_index("tp")
    c = lax.rem(ctx, NC)
    z = lax.rem(lax.div(ctx, NC), NZ)
    x = lax.div(ctx, GROUP)

    def at(xx, zz, cc):
        return {"ctx": (xx * NZ + zz) * NC + cc, "tp": y}

    def at_y(yy):
        return {"ctx": ctx, "tp": yy}

    def turn(v, by, n):
        return lax.rem(v + (by % n), n)

    ups = [at_y(turn(y, 1, NY)), at_y(turn(y, -1, NY))]
    sides = [at(turn(x, 1, NX), z, c), at(turn(x, -1, NX), z, c)]
    sib = at(x, z, 1 - c)

    barrier = pltpu.get_barrier_semaphore()
    greeted = (
        ups
        + [at(x, turn(z, d, NZ), c) for d in (4, 3, 5, 2, 6, 1, 7)]
        + [at(turn(x, d, NX), z, c) for d in (2, 1, 3)]
        + [sib]
    )
    for p in greeted:
        pl.semaphore_signal(barrier, inc=1, device_id=p, device_id_type=pl.DeviceIdType.MESH)

    loads = [
        pltpu.make_async_copy(src, dst, loc_sem.at[i])
        for i, (src, dst) in enumerate([
            (tok_ref, tok.at[y]),
            (wk_ref, w.at[x, z, c, 0]),
            (wv_ref, w.at[x, z, c, 1]),
            (wq_ref, w.at[x, z, c, 2]),
            (wo_ref, w.at[x, z, c, 3]),
            (feat_ref, feat),
        ])
    ]
    for copy in loads:
        copy.start()
    pl.semaphore_wait(barrier, len(greeted))

    sends = []

    def send(src, dst, rsem, dev):
        copy = pltpu.make_async_remote_copy(
            src_ref=src, dst_ref=dst, send_sem=ssem.at[len(sends)], recv_sem=rsem,
            device_id=dev, device_id_type=pl.DeviceIdType.MESH,
        )
        copy.start()
        sends.append(copy)

    def recv(dst, rsem):
        pltpu.make_async_copy(dst, dst, rsem).wait()

    def tok_owner(d, step):
        return turn(y, -step if d == 0 else step, NY)

    def tok_part(owner, r):
        return tok.at[owner, pl.ds(r * PIECE, PIECE)]

    def tok_send(d, step, r):
        part = tok_part(tok_owner(d, step), r)
        src = tok_ref.at[pl.ds(r * PIECE, PIECE)] if step == 0 else part
        send(src, part, tok_sem.at[d, step, r], ups[d])

    def tok_recv(d, step, r):
        recv(tok_part(tok_owner(d, step + 1), r), tok_sem.at[d, step, r])

    spans = (pl.ds(0, 2), pl.ds(2, 1), pl.ds(3, 1))

    def w_part(xx, zs, cc, part):
        return w.at[xx, zs, cc, spans[part]]

    def z_send(part):
        mine = w_part(x, z, c, part)
        for d in (4, 3, 5, 2, 6, 1, 7):
            send(mine, mine, z_sem.at[part, z], at(x, turn(z, d, NZ), c))

    def z_recv(part):
        for d in (1, 7, 2, 6, 3, 5, 4):
            zz = turn(z, d, NZ)
            recv(w_part(x, zz, c, part), z_sem.at[part, zz])

    every = pl.ds(0, NZ)
    halves = (pl.ds(0, NZ // 2), pl.ds(NZ // 2, NZ // 2))

    def sib_send(part, i, xx, zs):
        block = w_part(xx, zs, c, part)
        send(block, block, sib_sem.at[part, i], sib)

    def x_start(part):
        for i in range(2):
            for d in range(2):
                half = w_part(x, halves[d if i == 0 else 1 - d], c, part)
                send(half, half, x_sem.at[part, 2 * d + i], sides[d])
        sib_send(part, 0, x, every)

    def x_near(part, i):
        for d in range(2):
            xx = turn(x, -1 if d == 0 else 1, NX)
            zs = halves[d if i == 0 else 1 - d]
            half = w_part(xx, zs, c, part)
            recv(half, x_sem.at[part, 2 * d + i])
            if i == 0:
                send(half, half, x_sem.at[part, 4 + d], sides[d])
            sib_send(part, 1 + 2 * d + i, xx, zs)

    def x_far(part):
        xx = turn(x, 2, NX)
        for d in range(2):
            recv(w_part(xx, halves[d], c, part), x_sem.at[part, 4 + d])
            sib_send(part, 5 + d, xx, halves[d])

    def sib_recv(part):
        o = 1 - c
        recv(w_part(x, every, o, part), sib_sem.at[part, 0])
        for d in range(2):
            for i in range(2):
                xx = turn(x, -1 if d == 0 else 1, NX)
                recv(w_part(xx, halves[d if i == 0 else 1 - d], o, part), sib_sem.at[part, 1 + 2 * d + i])
            recv(w_part(turn(x, 2, NX), halves[d], o, part), sib_sem.at[part, 5 + d])

    for r in range(PIECES):
        for d in range(2):
            tok_send(d, 0, r)
    for copy in loads:
        copy.wait()
    z_send(0)

    for h in range(2):
        f = feat[h]
        hi = f.astype(BF)
        lo = (f - hi.astype(F32)).astype(BF)
        fcat[h] = jnp.concatenate([hi, hi, lo], axis=1)
        vaug[h, :, pl.ds(DH, DH)] = jnp.ones((TOK, DH), BF)

    def tok_pass(step, r):
        for d in range(2):
            tok_recv(d, step, r)
            tok_send(d, step + 1, r)

    for r in range(PIECES):
        tok_pass(0, r)
    z_recv(0)
    x_start(0)
    z_send(1)
    z_send(2)
    for r in range(PIECES):
        tok_pass(1, r)
    x_near(0, 0)
    for r in range(2):
        tok_recv(0, 2, r)
        tok_send(0, 3, r)
    x_near(0, 1)
    z_recv(1)
    x_start(1)
    for r in range(2, 4):
        tok_recv(1, 2, r)
        tok_send(1, 3, r)
    x_far(0)
    z_recv(2)
    sib_recv(0)

    def w_rows(s, k):
        return w[lax.div(s, 2), pl.ds(lax.rem(s, 2) * 4, 4), :, k].reshape(WIDTH, WIDTH)

    def kv_term(s, r):
        t = tok[s, pl.ds(r * HALF, HALF)]
        k = jnp.dot(t, w_rows(s, 0), preferred_element_type=F32)
        v = jnp.dot(t, w_rows(s, 1), preferred_element_type=F32)
        return k, v

    def kv_add(s):
        for r in range(2):
            k, v = kv_term(s, r)
            kv[0, pl.ds(r * HALF, HALF)] += k
            kv[1, pl.ds(r * HALF, HALF)] += v

    kv[...] = jnp.zeros_like(kv)

    @pl.loop(0, 5)
    def _(i):
        kv_add(lax.rem(y + i + (NY - 2), NY))

    x_near(1, 0)

    for r in range(2):
        tok_recv(0, 2, 2 + r)
        tok_recv(1, 2, r)

    @pl.loop(0, 2)
    def _(i):
        kv_add(lax.rem(y + 3 + 2 * i, NY))

    def positive(p, h):
        s = p * (DH ** -0.25)
        half_square = 0.5 * jnp.sum(s * s, axis=-1, keepdims=True)
        hi = s.astype(BF)
        lo = (s - hi.astype(F32)).astype(BF)
        logits = lax.dot_general(
            jnp.concatenate([hi, lo, hi], axis=1), fcat[h], NT, preferred_element_type=F32
        )
        return jnp.exp(logits - half_square).astype(BF)

    last = turn(y, 4, NY)

    def key_rows(r):
        rows_r = pl.ds(r * PIECE, PIECE)
        t = tok[last, rows_r]
        k = kv[0, rows_r] + jnp.dot(t, w_rows(last, 0), preferred_element_type=F32)
        v = kv[1, rows_r] + jnp.dot(t, w_rows(last, 1), preferred_element_type=F32)
        for h in range(2):
            phik[h, rows_r] = positive(k[:, h * DH : (h + 1) * DH], h)
            vaug[h, rows_r, pl.ds(0, DH)] = v[:, h * DH : (h + 1) * DH].astype(BF)

    def key_pair(p):
        tok_recv(0, 3, p)
        tok_recv(1, 3, 2 + p)
        key_rows(p)
        key_rows(2 + p)

    def key_sums(h, p):
        spans_p = [pl.ds(r * PIECE, PIECE) for r in (p, 2 + p)]
        return lax.dot_general(
            jnp.concatenate([vaug[h, rows_r] for rows_r in spans_p], axis=0),
            jnp.concatenate([phik[h, rows_r] for rows_r in spans_p], axis=0),
            TN, preferred_element_type=F32,
        )[:SROWS]

    key_pair(0)
    for h in range(2):
        sacc[h] = key_sums(h, 0)
    key_pair(1)
    ssend[...] = (sacc[1 - c] + key_sums(1 - c, 1)).astype(BF)
    send(ssend, srecv, j_sem.at[0], sib)
    own[...] = (sacc[c] + key_sums(c, 1)).astype(BF).astype(F32)
    recv(srecv, j_sem.at[0])
    chip = (own[...] + srecv[...].astype(F32)).astype(BF)
    tsend[...] = chip[:DH].reshape(NZ, SLICE, MF)
    nsend[...] = chip[DH:]

    for d in (4, 3, 5, 2, 6, 1, 7):
        zz = turn(z, d, NZ)
        send(tsend.at[zz], arecv.at[z], a_sem.at[z], at(x, zz, c))
    for d in (4, 3, 5, 2, 6, 1, 7):
        zz = turn(z, d, NZ)
        send(nsend, nrecv.at[z], an_sem.at[z], at(x, zz, c))
    arecv[z] = tsend[z]
    nrecv[z] = nsend[...]

    x_near(1, 1)
    x_start(2)
    x_far(1)
    sib_recv(1)

    @pl.loop(0, NY)
    def _(s):
        for r in range(2):
            t = tok[s, pl.ds(r * HALF, HALF)]
            term = jnp.dot(t, w_rows(s, 2), preferred_element_type=F32)
            rows_r = pl.ds(r * HALF, HALF)

            @pl.when(s == 0)
            def _():
                q[rows_r] = term

            @pl.when(s > 0)
            def _():
                q[rows_r] += term

    for d in (1, 7, 2, 6, 3, 5, 4):
        zz = turn(z, d, NZ)
        recv(arecv.at[zz], a_sem.at[zz])
    run = jnp.zeros((SLICE, MF), F32)
    for i in range(NZ):
        excl[i] = run
        run = run + arecv[i].astype(F32)
    tot[x] = run.astype(BF)
    for d in (2, 1, 3):
        send(tot.at[x], tot.at[x], b_sem.at[x], at(turn(x, d, NX), z, c))

    for d in (1, 7, 2, 6, 3, 5, 4):
        zz = turn(z, d, NZ)
        recv(nrecv.at[zz], an_sem.at[zz])
    run = jnp.zeros((SLICE, MF), F32)
    for i in range(NZ):
        run = run + nrecv[i].astype(F32)
    ntot[x] = run.astype(BF)
    for d in (2, 1, 3):
        send(ntot.at[x], ntot.at[x], bn_sem.at[x], at(turn(x, d, NX), z, c))

    def local(h):
        for r in range(2):
            rows_r = pl.ds(r * HALF, HALF)
            upto = (r + 1) * HALF
            sc = lax.dot_general(
                phiq[h, rows_r], phik[h, pl.ds(0, upto)], NT, preferred_element_type=F32
            )
            row = lax.broadcasted_iota(jnp.int32, (HALF, upto), 0) + r * HALF
            col = lax.broadcasted_iota(jnp.int32, (HALF, upto), 1)
            sc = jnp.where(col <= row, sc, 0.0).astype(BF)
            nd[h, rows_r] = jnp.dot(sc, vaug[h, pl.ds(0, upto)], preferred_element_type=F32)

    x_near(2, 0)
    for h in range(2):
        phiq[h] = positive(q[:, pl.ds(h * DH, DH)], h)
    local(0)

    for d in range(1, NX):
        xx = turn(x, d, NX)
        recv(tot.at[xx], b_sem.at[xx])
    base = jnp.zeros((SLICE, MF), F32)
    for i in range(NX):
        base = base + jnp.where(i < x, tot[i].astype(F32), 0.0)
    for i in range(NZ):
        psend[i] = (excl[i] + base).astype(BF)
    for d in (4, 3, 5, 2, 6, 1, 7):
        zz = turn(z, d, NZ)
        send(psend.at[zz], pfx.at[z], c_sem.at[z], at(x, zz, c))
    pfx[z] = psend[z]

    x_near(2, 1)
    local(1)
    x_far(2)
    sib_recv(2)

    for d in range(1, NX):
        xx = turn(x, d, NX)
        recv(ntot.at[xx], bn_sem.at[xx])
    base = jnp.zeros((SLICE, MF), F32)
    for i in range(NX):
        base = base + jnp.where(i < x, ntot[i].astype(F32), 0.0)
    for i in range(NZ):
        base = base + jnp.where(i < z, nrecv[i].astype(F32), 0.0)
    npre[...] = base

    for d in (1, 7, 2, 6, 3, 5, 4):
        zz = turn(z, d, NZ)
        recv(pfx.at[zz], c_sem.at[zz])

    before = jnp.concatenate([pfx[...].reshape(DH, MF).astype(F32), npre[...]], axis=0)
    fsend[...] = (before + jnp.where(c == 0, own[...], 0.0)).astype(BF)
    send(fsend, frecv, j_sem.at[1], sib)
    state = (before + jnp.where(c == 0, 0.0, srecv[...].astype(F32))).astype(BF)

    def spread(sums):
        return jnp.concatenate([sums[:DH]] + [sums[DH:]] * (DH // SLICE), axis=0)

    def finish(h, state, r):
        rows_r = pl.ds(r * HALF, HALF)
        full = nd[h, rows_r] + lax.dot_general(
            phiq[h, rows_r], state, NT, preferred_element_type=F32
        )
        head = pl.ds(pl.multiple_of(h * DH, DH), DH)
        attn[rows_r, head] = (full[:, :DH] / full[:, DH:]).astype(BF)

    def share(dest, r):
        return lax.dot_general(
            attn[pl.ds(r * PIECE, PIECE)], w_rows(dest, 3), NT, preferred_element_type=F32
        )

    def rs_item(d, step, r, first):
        dest = turn(y, (4 - step) if d == 0 else (step - 4), NY)
        value = share(dest, r)
        if not first:
            recv(rs_recv.at[d, step - 1, r], rs_sem.at[d, step - 1, r])
            value = value + rs_recv[d, step - 1, r].astype(F32)
        rs_send[d, step, r] = value.astype(BF)
        send(rs_send.at[d, step, r], rs_recv.at[d, step, r], rs_sem.at[d, step, r], ups[d])

    state = spread(state)
    finish(c, state, 0)
    finish(c, state, 1)
    recv(frecv, j_sem.at[1])
    state = spread(frecv[...])
    finish(1 - c, state, 0)
    for r in range(2):
        rs_item(0, 0, r, True)
    finish(1 - c, state, 1)
    for r in range(2):
        rs_item(1, 0, 2 + r, True)
    for step in range(1, 4):
        for k in range(4):
            for d in range(2):
                rs_item(d, step, (k + 2 * (1 - d)) % 4, step == 1 and k < 2)
    for r in range(PIECES):
        value = share(y, r)
        for d in range(2):
            recv(rs_recv.at[d, 3, r], rs_sem.at[d, 3, r])
            value = value + rs_recv[d, 3, r].astype(F32)
        out_ref[pl.ds(r * PIECE, PIECE)] = value.astype(BF)

    for copy in sends:
        copy.wait_send()


def body(tokens, w_query, w_key, w_value, features, w_out):
    hbm = pl.BlockSpec(memory_space=pl.ANY)
    dma = pltpu.SemaphoreType.DMA
    return pl.pallas_call(
        kernel,
        out_shape=jax.ShapeDtypeStruct((TOK, WIDTH), BF),
        in_specs=[hbm] * 6,
        out_specs=pl.BlockSpec(memory_space=pltpu.VMEM),
        scratch_shapes=[
            pltpu.VMEM((NY, TOK, WIDTH), BF),
            pltpu.VMEM((NX, NZ, NC, 4, SHARD, WIDTH), BF),
            pltpu.VMEM((2, TOK, WIDTH), F32),
            pltpu.VMEM((TOK, WIDTH), F32),
            pltpu.VMEM((2, TOK, 2 * DH), BF),
            pltpu.VMEM((2, TOK, MF), BF),
            pltpu.VMEM((2, TOK, MF), BF),
            pltpu.VMEM((2, MF, DH), F32),
            pltpu.VMEM((2, MF, 3 * DH), BF),
            pltpu.VMEM((2, TOK, 2 * DH), F32),
            pltpu.VMEM((2, SROWS, MF), F32),
            pltpu.VMEM((SROWS, MF), BF),
            pltpu.VMEM((SROWS, MF), BF),
            pltpu.VMEM((NZ, SLICE, MF), BF),
            pltpu.VMEM((NZ, SLICE, MF), BF),
            pltpu.VMEM((SLICE, MF), BF),
            pltpu.VMEM((NZ, SLICE, MF), BF),
            pltpu.VMEM((NZ, SLICE, MF), F32),
            pltpu.VMEM((NX, SLICE, MF), BF),
            pltpu.VMEM((NX, SLICE, MF), BF),
            pltpu.VMEM((NZ, SLICE, MF), BF),
            pltpu.VMEM((NZ, SLICE, MF), BF),
            pltpu.VMEM((SLICE, MF), F32),
            pltpu.VMEM((SROWS, MF), BF),
            pltpu.VMEM((SROWS, MF), BF),
            pltpu.VMEM((SROWS, MF), F32),
            pltpu.VMEM((TOK, 2 * DH), BF),
            pltpu.VMEM((2, 4, PIECES, PIECE, WIDTH), BF),
            pltpu.VMEM((2, 4, PIECES, PIECE, WIDTH), BF),
            dma((6,)),
            dma((SENDS,)),
            dma((2, 4, PIECES)),
            dma((3, NZ)),
            dma((3, 6)),
            dma((3, 7)),
            dma((NZ,)),
            dma((NZ,)),
            dma((NX,)),
            dma((NX,)),
            dma((NZ,)),
            dma((2,)),
            dma((2, 4, PIECES)),
        ],
        compiler_params=pltpu.CompilerParams(
            collective_id=0, has_side_effects=True, vmem_limit_bytes=56 * 1024 * 1024
        ),
    )(tokens, w_query, w_key, w_value, features, w_out.T)


def solution(mesh):
    return jax.shard_map(
        body,
        mesh=mesh,
        in_specs=(
            P("ctx", "tp"),
            P("ctx", "tp"),
            P("ctx", "tp"),
            P("ctx", "tp"),
            P("tp", None, None),
            P("tp", "ctx"),
        ),
        out_specs=P("ctx", "tp"),
        check_vma=False,
    )
```

```python
import jax
import jax.numpy as jnp
from jax import lax
from jax.experimental import pallas as pl
from jax.experimental.pallas import tpu as pltpu
from jax.sharding import PartitionSpec as P

NX, NZ, NC, NY = 4, 8, 2, 8
GROUP = NZ * NC
TOK = 512
HALF = 256
PIECES = 4
PIECE = 128
WIDTH = 256
DH = 128
MF = 256
SHARD = 32
SLICE = 16
SROWS = DH + SLICE
SENDS = 256
BF = jnp.bfloat16
F32 = jnp.float32
NT = (((1,), (1,)), ((), ()))
TN = (((0,), (0,)), ((), ()))


def kernel(
    tok_ref, wq_ref, wk_ref, wv_ref, feat_ref, wo_ref, out_ref,
    tok, w, kv, q, vaug, phik, phiq, feat, fcat, nd, sacc, ssend, srecv, tsend, arecv, nsend, nrecv,
    excl, tot, ntot, psend, pfx, npre, fsend, frecv, own, attn, rs_send, rs_recv,
    loc_sem, ssem, tok_sem, z_sem, n_sem, f_sem, k_sem, x_sem, sib_sem, a_sem, an_sem, b_sem, bn_sem, c_sem, j_sem, rs_sem,
):
    ctx = lax.axis_index("ctx")
    y = lax.axis_index("tp")
    c = lax.rem(ctx, NC)
    z = lax.rem(lax.div(ctx, NC), NZ)
    x = lax.div(ctx, GROUP)

    def at(xx, zz, cc):
        return {"ctx": (xx * NZ + zz) * NC + cc, "tp": y}

    def at_y(yy):
        return {"ctx": ctx, "tp": yy}

    def turn(v, by, n):
        return lax.rem(v + (by % n), n)

    ups = [at_y(turn(y, 1, NY)), at_y(turn(y, -1, NY))]
    sides = [at(turn(x, 1, NX), z, c), at(turn(x, -1, NX), z, c)]
    sib = at(x, z, 1 - c)

    barrier = pltpu.get_barrier_semaphore()
    greeted = (
        ups
        + [at(x, turn(z, d, NZ), c) for d in (4, 3, 5, 2, 6, 1, 7)]
        + [at(turn(x, d, NX), z, c) for d in (2, 1, 3)]
        + [sib]
    )
    for p in greeted:
        pl.semaphore_signal(barrier, inc=1, device_id=p, device_id_type=pl.DeviceIdType.MESH)

    loads = [
        pltpu.make_async_copy(src, dst, loc_sem.at[i])
        for i, (src, dst) in enumerate([
            (tok_ref, tok.at[y]),
            (wk_ref, w.at[x, z, c, 0]),
            (wv_ref, w.at[x, z, c, 1]),
            (wq_ref, w.at[x, z, c, 2]),
            (wo_ref, w.at[x, z, c, 3]),
            (feat_ref, feat),
        ])
    ]
    for copy in loads:
        copy.start()
    pl.semaphore_wait(barrier, len(greeted))

    sends = []

    def send(src, dst, rsem, dev):
        copy = pltpu.make_async_remote_copy(
            src_ref=src, dst_ref=dst, send_sem=ssem.at[len(sends)], recv_sem=rsem,
            device_id=dev, device_id_type=pl.DeviceIdType.MESH,
        )
        copy.start()
        sends.append(copy)

    def recv(dst, rsem):
        pltpu.make_async_copy(dst, dst, rsem).wait()

    def tok_owner(d, step):
        return turn(y, -step if d == 0 else step, NY)

    def tok_part(owner, r):
        return tok.at[owner, pl.ds(r * PIECE, PIECE)]

    def tok_send(d, step, r):
        part = tok_part(tok_owner(d, step), r)
        src = tok_ref.at[pl.ds(r * PIECE, PIECE)] if step == 0 else part
        send(src, part, tok_sem.at[d, step, r], ups[d])

    def tok_recv(d, step, r):
        recv(tok_part(tok_owner(d, step + 1), r), tok_sem.at[d, step, r])

    spans = (pl.ds(0, 2), pl.ds(2, 1), pl.ds(3, 1))

    def w_part(xx, zs, cc, part):
        return w.at[xx, zs, cc, spans[part]]

    def z_send(part):
        mine = w_part(x, z, c, part)
        for d in (1, 7, 2, 6, 3, 5, 4):
            send(mine, mine, z_sem.at[part, z], at(x, turn(z, d, NZ), c))

    def z_recv(part):
        for d in (1, 7, 2, 6, 3, 5, 4):
            zz = turn(z, d, NZ)
            recv(w_part(x, zz, c, part), z_sem.at[part, zz])

    every = pl.ds(0, NZ)
    halves = (pl.ds(0, NZ // 2), pl.ds(NZ // 2, NZ // 2))

    def sib_send(part, i, xx, zs):
        block = w_part(xx, zs, c, part)
        send(block, block, sib_sem.at[part, i], sib)

    def x_start(part):
        for i in range(2):
            for d in range(2):
                half = w_part(x, halves[d if i == 0 else 1 - d], c, part)
                send(half, half, x_sem.at[part, 2 * d + i], sides[d])
        sib_send(part, 0, x, every)

    def x_near(part, i):
        for d in range(2):
            xx = turn(x, -1 if d == 0 else 1, NX)
            zs = halves[d if i == 0 else 1 - d]
            half = w_part(xx, zs, c, part)
            recv(half, x_sem.at[part, 2 * d + i])
            if i == 0:
                send(half, half, x_sem.at[part, 4 + d], sides[d])
            sib_send(part, 1 + 2 * d + i, xx, zs)

    def x_far(part):
        xx = turn(x, 2, NX)
        for d in range(2):
            recv(w_part(xx, halves[d], c, part), x_sem.at[part, 4 + d])
            sib_send(part, 5 + d, xx, halves[d])

    def sib_recv(part):
        o = 1 - c
        recv(w_part(x, every, o, part), sib_sem.at[part, 0])
        for d in range(2):
            for i in range(2):
                xx = turn(x, -1 if d == 0 else 1, NX)
                recv(w_part(xx, halves[d if i == 0 else 1 - d], o, part), sib_sem.at[part, 1 + 2 * d + i])
            recv(w_part(turn(x, 2, NX), halves[d], o, part), sib_sem.at[part, 5 + d])

    def one(xx, off, cc):
        return w_part(xx, turn(z, off, NZ), cc, 0)

    def near_send(offs):
        for o in offs:
            shard = one(x, o, c)
            for d in range(2):
                send(shard, shard, n_sem.at[d, o], sides[d])
            send(shard, shard, k_sem.at[0, o], sib)

    def z_group(offs):
        for o in offs:
            recv(one(x, o, c), z_sem.at[0, turn(z, o, NZ)])
        near_send(offs)

    def near_group(offs):
        for o in offs:
            for d in range(2):
                shard = one(turn(x, -1 if d == 0 else 1, NX), o, c)
                recv(shard, n_sem.at[d, o])
                if (o < NZ // 2) == (d == 0):
                    send(shard, shard, f_sem.at[o], sides[d])
                send(shard, shard, k_sem.at[1 + d, o], sib)

    def far_group(offs):
        for o in offs:
            shard = one(turn(x, 2, NX), o, c)
            recv(shard, f_sem.at[o])
            send(shard, shard, k_sem.at[3, o], sib)

    def key_weights():
        for i, by in enumerate((0, -1, 1, 2)):
            for o in range(NZ):
                recv(one(turn(x, by, NX), o, 1 - c), k_sem.at[i, o])

    for r in range(PIECES):
        for d in range(2):
            tok_send(d, 0, r)
    for copy in loads:
        copy.wait()
    z_send(0)
    near_send((0,))

    for h in range(2):
        f = feat[h]
        hi = f.astype(BF)
        lo = (f - hi.astype(F32)).astype(BF)
        fcat[h] = jnp.concatenate([hi, hi, lo], axis=1)
        vaug[h, :, pl.ds(DH, DH)] = jnp.ones((TOK, DH), BF)

    def tok_pass(step, r):
        for d in range(2):
            tok_recv(d, step, r)
            tok_send(d, step + 1, r)

    groups = ((0,), (1, 7), (2, 6), (3, 5, 4))
    tok_pass(0, 0)
    z_group(groups[1])
    tok_pass(0, 1)
    z_group(groups[2])
    near_group(groups[0])
    tok_pass(0, 2)
    z_group(groups[3])
    near_group(groups[1])
    z_send(1)
    z_send(2)
    tok_pass(0, 3)
    near_group(groups[2])
    tok_pass(1, 0)
    near_group(groups[3])
    far_group(groups[0])
    tok_pass(1, 1)
    far_group(groups[1])
    tok_pass(1, 2)
    far_group(groups[2])
    tok_pass(1, 3)
    far_group(groups[3])
    z_recv(1)
    x_start(1)
    for r in range(2):
        tok_recv(0, 2, r)
        tok_send(0, 3, r)
    key_weights()
    for r in range(2, 4):
        tok_recv(1, 2, r)
        tok_send(1, 3, r)
    z_recv(2)

    def w_rows(s, k):
        return w[lax.div(s, 2), pl.ds(lax.rem(s, 2) * 4, 4), :, k].reshape(WIDTH, WIDTH)

    def early(by, add):
        shards = [turn(y, d, NY) for d in by]

        @pl.loop(0, 2)
        def _(r):
            rows_r = pl.ds(pl.multiple_of(r * HALF, HALF), HALF)
            t = jnp.concatenate([tok[s, rows_r] for s in shards], axis=1)
            for k in range(2):
                wide = jnp.concatenate([w_rows(s, k) for s in shards], axis=0)
                value = jnp.dot(t, wide, preferred_element_type=F32)
                kv[k, rows_r] = kv[k, rows_r] + value if add else value

    early((0, 1, -1, 2, -2), False)
    x_near(1, 0)
    for r in range(2):
        tok_recv(0, 2, 2 + r)
        tok_recv(1, 2, r)
    early((3, -3), True)

    def positive(p, h):
        s = p * (DH ** -0.25)
        half_square = 0.5 * jnp.sum(s * s, axis=-1, keepdims=True)
        hi = s.astype(BF)
        lo = (s - hi.astype(F32)).astype(BF)
        logits = lax.dot_general(
            jnp.concatenate([hi, lo, hi], axis=1), fcat[h], NT, preferred_element_type=F32
        )
        return jnp.exp(logits - half_square).astype(BF)

    last = turn(y, 4, NY)

    def key_rows(r):
        rows_r = pl.ds(r * PIECE, PIECE)
        t = tok[last, rows_r]
        k = kv[0, rows_r] + jnp.dot(t, w_rows(last, 0), preferred_element_type=F32)
        v = kv[1, rows_r] + jnp.dot(t, w_rows(last, 1), preferred_element_type=F32)
        for h in range(2):
            phik[h, rows_r] = positive(k[:, h * DH : (h + 1) * DH], h)
            vaug[h, rows_r, pl.ds(0, DH)] = v[:, h * DH : (h + 1) * DH].astype(BF)

    def key_pair(p):
        tok_recv(0, 3, p)
        tok_recv(1, 3, 2 + p)
        key_rows(p)
        key_rows(2 + p)

    def key_sums(h, p):
        spans_p = [pl.ds(r * PIECE, PIECE) for r in (p, 2 + p)]
        return lax.dot_general(
            jnp.concatenate([vaug[h, rows_r] for rows_r in spans_p], axis=0),
            jnp.concatenate([phik[h, rows_r] for rows_r in spans_p], axis=0),
            TN, preferred_element_type=F32,
        )[:SROWS]

    key_pair(0)
    for h in range(2):
        sacc[h] = key_sums(h, 0)
    key_pair(1)
    ssend[...] = (sacc[1 - c] + key_sums(1 - c, 1)).astype(BF)
    send(ssend, srecv, j_sem.at[0], sib)
    own[...] = (sacc[c] + key_sums(c, 1)).astype(BF).astype(F32)
    recv(srecv, j_sem.at[0])
    chip = (own[...] + srecv[...].astype(F32)).astype(BF)
    tsend[...] = chip[:DH].reshape(NZ, SLICE, MF)
    nsend[...] = chip[DH:]

    for d in (4, 3, 5, 2, 6, 1, 7):
        zz = turn(z, d, NZ)
        send(tsend.at[zz], arecv.at[z], a_sem.at[z], at(x, zz, c))
    for d in (4, 3, 5, 2, 6, 1, 7):
        zz = turn(z, d, NZ)
        send(nsend, nrecv.at[z], an_sem.at[z], at(x, zz, c))
    arecv[z] = tsend[z]
    nrecv[z] = nsend[...]

    x_near(1, 1)
    x_start(2)
    x_far(1)
    sib_recv(1)

    @pl.loop(0, 2)
    def _(r):
        rows_r = pl.ds(pl.multiple_of(r * HALF, HALF), HALF)
        t = jnp.concatenate([tok[s, rows_r] for s in range(NY)], axis=1)
        q[rows_r] = jnp.dot(
            t, w[:, :, :, 2].reshape(NY * WIDTH, WIDTH), preferred_element_type=F32
        )

    for d in (1, 7, 2, 6, 3, 5, 4):
        zz = turn(z, d, NZ)
        recv(arecv.at[zz], a_sem.at[zz])
    run = jnp.zeros((SLICE, MF), F32)
    for i in range(NZ):
        excl[i] = run
        run = run + arecv[i].astype(F32)
    tot[x] = run.astype(BF)
    for d in (2, 1, 3):
        send(tot.at[x], tot.at[x], b_sem.at[x], at(turn(x, d, NX), z, c))

    for d in (1, 7, 2, 6, 3, 5, 4):
        zz = turn(z, d, NZ)
        recv(nrecv.at[zz], an_sem.at[zz])
    run = jnp.zeros((SLICE, MF), F32)
    for i in range(NZ):
        run = run + nrecv[i].astype(F32)
    ntot[x] = run.astype(BF)
    for d in (2, 1, 3):
        send(ntot.at[x], ntot.at[x], bn_sem.at[x], at(turn(x, d, NX), z, c))

    def local(h):
        for r in range(2):
            rows_r = pl.ds(r * HALF, HALF)
            upto = (r + 1) * HALF
            sc = lax.dot_general(
                phiq[h, rows_r], phik[h, pl.ds(0, upto)], NT, preferred_element_type=F32
            )
            row = lax.broadcasted_iota(jnp.int32, (HALF, upto), 0) + r * HALF
            col = lax.broadcasted_iota(jnp.int32, (HALF, upto), 1)
            sc = jnp.where(col <= row, sc, 0.0).astype(BF)
            nd[h, rows_r] = jnp.dot(sc, vaug[h, pl.ds(0, upto)], preferred_element_type=F32)

    x_near(2, 0)
    for h in range(2):
        phiq[h] = positive(q[:, pl.ds(h * DH, DH)], h)
    local(0)

    for d in range(1, NX):
        xx = turn(x, d, NX)
        recv(tot.at[xx], b_sem.at[xx])
    base = jnp.zeros((SLICE, MF), F32)
    for i in range(NX):
        base = base + jnp.where(i < x, tot[i].astype(F32), 0.0)
    for i in range(NZ):
        psend[i] = (excl[i] + base).astype(BF)
    for d in (4, 3, 5, 2, 6, 1, 7):
        zz = turn(z, d, NZ)
        send(psend.at[zz], pfx.at[z], c_sem.at[z], at(x, zz, c))
    pfx[z] = psend[z]

    x_near(2, 1)
    local(1)
    x_far(2)
    sib_recv(2)

    for d in range(1, NX):
        xx = turn(x, d, NX)
        recv(ntot.at[xx], bn_sem.at[xx])
    base = jnp.zeros((SLICE, MF), F32)
    for i in range(NX):
        base = base + jnp.where(i < x, ntot[i].astype(F32), 0.0)
    for i in range(NZ):
        base = base + jnp.where(i < z, nrecv[i].astype(F32), 0.0)
    npre[...] = base

    for d in (1, 7, 2, 6, 3, 5, 4):
        zz = turn(z, d, NZ)
        recv(pfx.at[zz], c_sem.at[zz])

    before = jnp.concatenate([pfx[...].reshape(DH, MF).astype(F32), npre[...]], axis=0)
    fsend[...] = (before + jnp.where(c == 0, own[...], 0.0)).astype(BF)
    send(fsend, frecv, j_sem.at[1], sib)
    state = (before + jnp.where(c == 0, 0.0, srecv[...].astype(F32))).astype(BF)

    def spread(sums):
        return jnp.concatenate([sums[:DH]] + [sums[DH:]] * (DH // SLICE), axis=0)

    def finish(h, state, r):
        rows_r = pl.ds(r * HALF, HALF)
        full = nd[h, rows_r] + lax.dot_general(
            phiq[h, rows_r], state, NT, preferred_element_type=F32
        )
        head = pl.ds(pl.multiple_of(h * DH, DH), DH)
        attn[rows_r, head] = (full[:, :DH] / full[:, DH:]).astype(BF)

    def share(dest, r):
        return lax.dot_general(
            attn[pl.ds(r * PIECE, PIECE)], w_rows(dest, 3), NT, preferred_element_type=F32
        )

    def rs_item(d, step, r, first):
        dest = turn(y, (4 - step) if d == 0 else (step - 4), NY)
        value = share(dest, r)
        if not first:
            recv(rs_recv.at[d, step - 1, r], rs_sem.at[d, step - 1, r])
            value = value + rs_recv[d, step - 1, r].astype(F32)
        rs_send[d, step, r] = value.astype(BF)
        send(rs_send.at[d, step, r], rs_recv.at[d, step, r], rs_sem.at[d, step, r], ups[d])

    state = spread(state)
    finish(c, state, 0)
    finish(c, state, 1)
    recv(frecv, j_sem.at[1])
    state = spread(frecv[...])
    finish(1 - c, state, 0)
    for r in range(2):
        rs_item(0, 0, r, True)
    finish(1 - c, state, 1)
    for r in range(2):
        rs_item(1, 0, 2 + r, True)
    for step in range(1, 4):
        for k in range(4):
            for d in range(2):
                rs_item(d, step, (k + 2 * (1 - d)) % 4, step == 1 and k < 2)
    for r in range(PIECES):
        value = share(y, r)
        for d in range(2):
            recv(rs_recv.at[d, 3, r], rs_sem.at[d, 3, r])
            value = value + rs_recv[d, 3, r].astype(F32)
        out_ref[pl.ds(r * PIECE, PIECE)] = value.astype(BF)

    for copy in sends:
        copy.wait_send()


def body(tokens, w_query, w_key, w_value, features, w_out):
    hbm = pl.BlockSpec(memory_space=pl.ANY)
    dma = pltpu.SemaphoreType.DMA
    return pl.pallas_call(
        kernel,
        out_shape=jax.ShapeDtypeStruct((TOK, WIDTH), BF),
        in_specs=[hbm] * 6,
        out_specs=pl.BlockSpec(memory_space=pltpu.VMEM),
        scratch_shapes=[
            pltpu.VMEM((NY, TOK, WIDTH), BF),
            pltpu.VMEM((NX, NZ, NC, 4, SHARD, WIDTH), BF),
            pltpu.VMEM((2, TOK, WIDTH), F32),
            pltpu.VMEM((TOK, WIDTH), F32),
            pltpu.VMEM((2, TOK, 2 * DH), BF),
            pltpu.VMEM((2, TOK, MF), BF),
            pltpu.VMEM((2, TOK, MF), BF),
            pltpu.VMEM((2, MF, DH), F32),
            pltpu.VMEM((2, MF, 3 * DH), BF),
            pltpu.VMEM((2, TOK, 2 * DH), F32),
            pltpu.VMEM((2, SROWS, MF), F32),
            pltpu.VMEM((SROWS, MF), BF),
            pltpu.VMEM((SROWS, MF), BF),
            pltpu.VMEM((NZ, SLICE, MF), BF),
            pltpu.VMEM((NZ, SLICE, MF), BF),
            pltpu.VMEM((SLICE, MF), BF),
            pltpu.VMEM((NZ, SLICE, MF), BF),
            pltpu.VMEM((NZ, SLICE, MF), F32),
            pltpu.VMEM((NX, SLICE, MF), BF),
            pltpu.VMEM((NX, SLICE, MF), BF),
            pltpu.VMEM((NZ, SLICE, MF), BF),
            pltpu.VMEM((NZ, SLICE, MF), BF),
            pltpu.VMEM((SLICE, MF), F32),
            pltpu.VMEM((SROWS, MF), BF),
            pltpu.VMEM((SROWS, MF), BF),
            pltpu.VMEM((SROWS, MF), F32),
            pltpu.VMEM((TOK, 2 * DH), BF),
            pltpu.VMEM((2, 4, PIECES, PIECE, WIDTH), BF),
            pltpu.VMEM((2, 4, PIECES, PIECE, WIDTH), BF),
            dma((6,)),
            dma((SENDS,)),
            dma((2, 4, PIECES)),
            dma((3, NZ)),
            dma((2, NZ)),
            dma((NZ,)),
            dma((4, NZ)),
            dma((3, 6)),
            dma((3, 7)),
            dma((NZ,)),
            dma((NZ,)),
            dma((NX,)),
            dma((NX,)),
            dma((NZ,)),
            dma((2,)),
            dma((2, 4, PIECES)),
        ],
        compiler_params=pltpu.CompilerParams(
            collective_id=0, has_side_effects=True, vmem_limit_bytes=56 * 1024 * 1024
        ),
    )(tokens, w_query, w_key, w_value, features, w_out.T)


def solution(mesh):
    return jax.shard_map(
        body,
        mesh=mesh,
        in_specs=(
            P("ctx", "tp"),
            P("ctx", "tp"),
            P("ctx", "tp"),
            P("ctx", "tp"),
            P("tp", None, None),
            P("tp", "ctx"),
        ),
        out_specs=P("ctx", "tp"),
        check_vma=False,
    )
```

```python
import jax
import jax.numpy as jnp
from jax import lax
from jax.experimental import pallas as pl
from jax.experimental.pallas import tpu as pltpu
from jax.sharding import PartitionSpec as P

NX, NZ, NC, NY = 4, 8, 2, 8
GROUP = NZ * NC
TOK = 512
HALF = 256
PIECES = 4
PIECE = 128
WIDTH = 256
DH = 128
MF = 256
SHARD = 32
SLICE = 16
SROWS = DH + SLICE
SENDS = 192
BF = jnp.bfloat16
F32 = jnp.float32
NT = (((1,), (1,)), ((), ()))
TN = (((0,), (0,)), ((), ()))


def kernel(
    tok_ref, wq_ref, wk_ref, wv_ref, feat_ref, wo_ref, out_ref,
    tok, w, kv, q, vaug, phik, phiq, feat, fcat, nd, sacc, ssend, srecv, tsend, arecv, nsend, nrecv,
    excl, tot, ntot, psend, pfx, npre, fsend, frecv, own, attn, rs_send, rs_recv, result,
    loc_sem, ssem, tok_sem, z_sem, x_sem, sib_sem, a_sem, an_sem, b_sem, bn_sem, c_sem, j_sem, rs_sem,
):
    ctx = lax.axis_index("ctx")
    y = lax.axis_index("tp")
    c = lax.rem(ctx, NC)
    z = lax.rem(lax.div(ctx, NC), NZ)
    x = lax.div(ctx, GROUP)

    def at(xx, zz, cc):
        return {"ctx": (xx * NZ + zz) * NC + cc, "tp": y}

    def at_y(yy):
        return {"ctx": ctx, "tp": yy}

    def turn(v, by, n):
        return lax.rem(v + (by % n), n)

    ups = [at_y(turn(y, 1, NY)), at_y(turn(y, -1, NY))]
    sides = [at(turn(x, 1, NX), z, c), at(turn(x, -1, NX), z, c)]
    sib = at(x, z, 1 - c)

    barrier = pltpu.get_barrier_semaphore()
    greeted = (
        ups
        + [at(x, turn(z, d, NZ), c) for d in (4, 3, 5, 2, 6, 1, 7)]
        + [at(turn(x, d, NX), z, c) for d in (2, 1, 3)]
        + [sib]
    )
    for p in greeted:
        pl.semaphore_signal(barrier, inc=1, device_id=p, device_id_type=pl.DeviceIdType.MESH)

    loads = [
        pltpu.make_async_copy(src, dst, loc_sem.at[i])
        for i, (src, dst) in enumerate([
            (tok_ref, tok.at[y]),
            (wk_ref, w.at[x, z, c, 0]),
            (wv_ref, w.at[x, z, c, 1]),
            (wq_ref, w.at[x, z, c, 2]),
            (wo_ref, w.at[x, z, c, 3]),
            (feat_ref, feat),
        ])
    ]
    for copy in loads:
        copy.start()
    pl.semaphore_wait(barrier, len(greeted))

    sends = []

    def send(src, dst, rsem, dev):
        copy = pltpu.make_async_remote_copy(
            src_ref=src, dst_ref=dst, send_sem=ssem.at[len(sends)], recv_sem=rsem,
            device_id=dev, device_id_type=pl.DeviceIdType.MESH,
        )
        copy.start()
        sends.append(copy)

    def recv(dst, rsem):
        pltpu.make_async_copy(dst, dst, rsem).wait()

    def tok_owner(d, step):
        return turn(y, -step if d == 0 else step, NY)

    def tok_part(owner, r):
        return tok.at[owner, pl.ds(r * PIECE, PIECE)]

    def tok_send(d, step, r):
        part = tok_part(tok_owner(d, step), r)
        src = tok_ref.at[pl.ds(r * PIECE, PIECE)] if step == 0 else part
        send(src, part, tok_sem.at[d, step, r], ups[d])

    def tok_recv(d, step, r):
        recv(tok_part(tok_owner(d, step + 1), r), tok_sem.at[d, step, r])

    spans = (pl.ds(0, 2), pl.ds(2, 1), pl.ds(3, 1))

    def w_part(xx, zs, cc, part):
        return w.at[xx, zs, cc, spans[part]]

    def z_send(part):
        mine = w_part(x, z, c, part)
        for d in (4, 3, 5, 2, 6, 1, 7):
            send(mine, mine, z_sem.at[part, z], at(x, turn(z, d, NZ), c))

    def z_recv(part):
        for d in (1, 7, 2, 6, 3, 5, 4):
            zz = turn(z, d, NZ)
            recv(w_part(x, zz, c, part), z_sem.at[part, zz])

    every = pl.ds(0, NZ)
    halves = (pl.ds(0, NZ // 2), pl.ds(NZ // 2, NZ // 2))

    def sib_send(part, i, xx, zs):
        block = w_part(xx, zs, c, part)
        send(block, block, sib_sem.at[part, i], sib)

    def x_start(part):
        for i in range(2):
            for d in range(2):
                half = w_part(x, halves[d if i == 0 else 1 - d], c, part)
                send(half, half, x_sem.at[part, 2 * d + i], sides[d])
        sib_send(part, 0, x, every)

    def x_near(part, i):
        for d in range(2):
            xx = turn(x, -1 if d == 0 else 1, NX)
            zs = halves[d if i == 0 else 1 - d]
            half = w_part(xx, zs, c, part)
            recv(half, x_sem.at[part, 2 * d + i])
            if i == 0:
                send(half, half, x_sem.at[part, 4 + d], sides[d])
            sib_send(part, 1 + 2 * d + i, xx, zs)

    def x_far(part):
        xx = turn(x, 2, NX)
        for d in range(2):
            recv(w_part(xx, halves[d], c, part), x_sem.at[part, 4 + d])
            sib_send(part, 5 + d, xx, halves[d])

    def sib_recv(part):
        o = 1 - c
        recv(w_part(x, every, o, part), sib_sem.at[part, 0])
        for d in range(2):
            for i in range(2):
                xx = turn(x, -1 if d == 0 else 1, NX)
                recv(w_part(xx, halves[d if i == 0 else 1 - d], o, part), sib_sem.at[part, 1 + 2 * d + i])
            recv(w_part(turn(x, 2, NX), halves[d], o, part), sib_sem.at[part, 5 + d])

    for r in range(PIECES):
        for d in range(2):
            tok_send(d, 0, r)
    for copy in loads:
        copy.wait()
    z_send(0)

    for h in range(2):
        f = feat[h]
        hi = f.astype(BF)
        lo = (f - hi.astype(F32)).astype(BF)
        fcat[h] = jnp.concatenate([hi, hi, lo], axis=1)
        vaug[h, :, pl.ds(DH, DH)] = jnp.ones((TOK, DH), BF)

    def tok_pass(step, r):
        for d in range(2):
            tok_recv(d, step, r)
            tok_send(d, step + 1, r)

    for r in range(PIECES):
        tok_pass(0, r)
    z_recv(0)
    x_start(0)
    z_send(1)
    z_send(2)
    for r in range(PIECES):
        tok_pass(1, r)
    x_near(0, 0)
    for r in range(2):
        tok_recv(0, 2, r)
        tok_send(0, 3, r)
    x_near(0, 1)
    z_recv(1)
    x_start(1)
    for r in range(2, 4):
        tok_recv(1, 2, r)
        tok_send(1, 3, r)
    x_far(0)
    z_recv(2)
    sib_recv(0)

    def w_rows(s, k):
        return w[lax.div(s, 2), pl.ds(lax.rem(s, 2) * 4, 4), :, k].reshape(WIDTH, WIDTH)

    for r in range(2):
        tok_recv(0, 2, 2 + r)
        tok_recv(1, 2, r)

    early = [turn(y, d, NY) for d in (0, 1, -1, 2, -2, 3, -3)]

    @pl.loop(0, 2)
    def _(r):
        rows_r = pl.ds(pl.multiple_of(r * HALF, HALF), HALF)
        t = jnp.concatenate([tok[s, rows_r] for s in early], axis=1)
        for k in range(2):
            wide = jnp.concatenate([w_rows(s, k) for s in early], axis=0)
            kv[k, rows_r] = jnp.dot(t, wide, preferred_element_type=F32)

    x_near(1, 0)

    def positive(p, h):
        s = p * (DH ** -0.25)
        half_square = 0.5 * jnp.sum(s * s, axis=-1, keepdims=True)
        hi = s.astype(BF)
        lo = (s - hi.astype(F32)).astype(BF)
        logits = lax.dot_general(
            jnp.concatenate([hi, lo, hi], axis=1), fcat[h], NT, preferred_element_type=F32
        )
        return jnp.exp(logits - half_square).astype(BF)

    last = turn(y, 4, NY)

    def key_rows(r):
        rows_r = pl.ds(r * PIECE, PIECE)
        t = tok[last, rows_r]
        k = kv[0, rows_r] + jnp.dot(t, w_rows(last, 0), preferred_element_type=F32)
        v = kv[1, rows_r] + jnp.dot(t, w_rows(last, 1), preferred_element_type=F32)
        for h in range(2):
            phik[h, rows_r] = positive(k[:, h * DH : (h + 1) * DH], h)
            vaug[h, rows_r, pl.ds(0, DH)] = v[:, h * DH : (h + 1) * DH].astype(BF)

    def key_pair(p):
        tok_recv(0, 3, p)
        tok_recv(1, 3, 2 + p)
        key_rows(p)
        key_rows(2 + p)

    def key_sums(h, p):
        spans_p = [pl.ds(r * PIECE, PIECE) for r in (p, 2 + p)]
        return lax.dot_general(
            jnp.concatenate([vaug[h, rows_r] for rows_r in spans_p], axis=0),
            jnp.concatenate([phik[h, rows_r] for rows_r in spans_p], axis=0),
            TN, preferred_element_type=F32,
        )[:SROWS]

    key_pair(0)
    for h in range(2):
        sacc[h] = key_sums(h, 0)
    key_pair(1)
    ssend[...] = (sacc[1 - c] + key_sums(1 - c, 1)).astype(BF)
    send(ssend, srecv, j_sem.at[0], sib)
    own[...] = (sacc[c] + key_sums(c, 1)).astype(BF).astype(F32)
    recv(srecv, j_sem.at[0])
    chip = (own[...] + srecv[...].astype(F32)).astype(BF)
    tsend[...] = chip[:DH].reshape(NZ, SLICE, MF)
    nsend[...] = chip[DH:]

    for d in (4, 3, 5, 2, 6, 1, 7):
        zz = turn(z, d, NZ)
        send(tsend.at[zz], arecv.at[z], a_sem.at[z], at(x, zz, c))
    for d in (4, 3, 5, 2, 6, 1, 7):
        zz = turn(z, d, NZ)
        send(nsend, nrecv.at[z], an_sem.at[z], at(x, zz, c))
    arecv[z] = tsend[z]
    nrecv[z] = nsend[...]

    x_near(1, 1)
    x_start(2)
    x_far(1)
    sib_recv(1)

    @pl.loop(0, 2)
    def _(r):
        rows_r = pl.ds(pl.multiple_of(r * HALF, HALF), HALF)
        t = jnp.concatenate([tok[s, rows_r] for s in range(NY)], axis=1)
        q[rows_r] = jnp.dot(
            t, w[:, :, :, 2].reshape(NY * WIDTH, WIDTH), preferred_element_type=F32
        )

    for d in (1, 7, 2, 6, 3, 5, 4):
        zz = turn(z, d, NZ)
        recv(arecv.at[zz], a_sem.at[zz])
    run = jnp.zeros((SLICE, MF), F32)
    for i in range(NZ):
        excl[i] = run
        run = run + arecv[i].astype(F32)
    tot[x] = run.astype(BF)
    for d in (2, 1, 3):
        send(tot.at[x], tot.at[x], b_sem.at[x], at(turn(x, d, NX), z, c))

    for d in (1, 7, 2, 6, 3, 5, 4):
        zz = turn(z, d, NZ)
        recv(nrecv.at[zz], an_sem.at[zz])
    run = jnp.zeros((SLICE, MF), F32)
    for i in range(NZ):
        run = run + nrecv[i].astype(F32)
    ntot[x] = run.astype(BF)
    for d in (2, 1, 3):
        send(ntot.at[x], ntot.at[x], bn_sem.at[x], at(turn(x, d, NX), z, c))

    def local(h):
        for r in range(2):
            rows_r = pl.ds(r * HALF, HALF)
            upto = (r + 1) * HALF
            sc = lax.dot_general(
                phiq[h, rows_r], phik[h, pl.ds(0, upto)], NT, preferred_element_type=F32
            )
            row = lax.broadcasted_iota(jnp.int32, (HALF, upto), 0) + r * HALF
            col = lax.broadcasted_iota(jnp.int32, (HALF, upto), 1)
            sc = jnp.where(col <= row, sc, 0.0).astype(BF)
            nd[h, rows_r] = jnp.dot(sc, vaug[h, pl.ds(0, upto)], preferred_element_type=F32)

    x_near(2, 0)
    for h in range(2):
        phiq[h] = positive(q[:, pl.ds(h * DH, DH)], h)
    local(0)

    for d in range(1, NX):
        xx = turn(x, d, NX)
        recv(tot.at[xx], b_sem.at[xx])
    base = jnp.zeros((SLICE, MF), F32)
    for i in range(NX):
        base = base + jnp.where(i < x, tot[i].astype(F32), 0.0)
    for i in range(NZ):
        psend[i] = (excl[i] + base).astype(BF)
    for d in (4, 3, 5, 2, 6, 1, 7):
        zz = turn(z, d, NZ)
        send(psend.at[zz], pfx.at[z], c_sem.at[z], at(x, zz, c))
    pfx[z] = psend[z]

    x_near(2, 1)
    local(1)
    x_far(2)
    sib_recv(2)

    for d in range(1, NX):
        xx = turn(x, d, NX)
        recv(ntot.at[xx], bn_sem.at[xx])
    base = jnp.zeros((SLICE, MF), F32)
    for i in range(NX):
        base = base + jnp.where(i < x, ntot[i].astype(F32), 0.0)
    for i in range(NZ):
        base = base + jnp.where(i < z, nrecv[i].astype(F32), 0.0)
    npre[...] = base

    for d in (1, 7, 2, 6, 3, 5, 4):
        zz = turn(z, d, NZ)
        recv(pfx.at[zz], c_sem.at[zz])

    before = jnp.concatenate([pfx[...].reshape(DH, MF).astype(F32), npre[...]], axis=0)
    fsend[...] = (before + jnp.where(c == 0, own[...], 0.0)).astype(BF)
    send(fsend, frecv, j_sem.at[1], sib)
    state = (before + jnp.where(c == 0, 0.0, srecv[...].astype(F32))).astype(BF)

    def spread(sums):
        return jnp.concatenate([sums[:DH]] + [sums[DH:]] * (DH // SLICE), axis=0)

    def finish(h, state, r):
        rows_r = pl.ds(r * HALF, HALF)
        full = nd[h, rows_r] + lax.dot_general(
            phiq[h, rows_r], state, NT, preferred_element_type=F32
        )
        head = pl.ds(pl.multiple_of(h * DH, DH), DH)
        attn[rows_r, head] = (full[:, :DH] / full[:, DH:]).astype(BF)

    def share(dest, r):
        return lax.dot_general(
            attn[pl.ds(r * PIECE, PIECE)], w_rows(dest, 3), NT, preferred_element_type=F32
        )

    def rs_item(d, step, r, first):
        dest = turn(y, (4 - step) if d == 0 else (step - 4), NY)
        value = share(dest, r)
        if not first:
            recv(rs_recv.at[d, step - 1, r], rs_sem.at[d, step - 1, r])
            value = value + rs_recv[d, step - 1, r].astype(F32)
        rs_send[d, step, r] = value.astype(BF)
        send(rs_send.at[d, step, r], rs_recv.at[d, step, r], rs_sem.at[d, step, r], ups[d])

    before_ring = len(sends)
    waited = []

    def drain(count, stop):
        for copy in sends[len(waited) : min(len(waited) + count, stop)]:
            copy.wait_send()
            waited.append(copy)

    state = spread(state)
    finish(c, state, 0)
    finish(c, state, 1)
    recv(frecv, j_sem.at[1])
    state = spread(frecv[...])
    finish(1 - c, state, 0)
    for r in range(2):
        rs_item(0, 0, r, True)
    finish(1 - c, state, 1)
    for r in range(2):
        rs_item(1, 0, 2 + r, True)
    for step in range(1, 4):
        for k in range(4):
            for d in range(2):
                rs_item(d, step, (k + 2 * (1 - d)) % 4, step == 1 and k < 2)
                drain(before_ring // 20, before_ring)
    drain(len(sends), len(sends) - 8)
    stores = []
    for r in range(PIECES):
        value = share(y, r)
        for d in range(2):
            recv(rs_recv.at[d, 3, r], rs_sem.at[d, 3, r])
            value = value + rs_recv[d, 3, r].astype(F32)
        rows_r = pl.ds(r * PIECE, PIECE)
        result[rows_r] = value.astype(BF)
        store = pltpu.make_async_copy(result.at[rows_r], out_ref.at[rows_r], loc_sem.at[r])
        store.start()
        stores.append(store)

    drain(len(sends), len(sends))
    for store in stores:
        store.wait()


def body(tokens, w_query, w_key, w_value, features, w_out):
    hbm = pl.BlockSpec(memory_space=pl.ANY)
    dma = pltpu.SemaphoreType.DMA
    return pl.pallas_call(
        kernel,
        out_shape=jax.ShapeDtypeStruct((TOK, WIDTH), BF),
        in_specs=[hbm] * 6,
        out_specs=hbm,
        scratch_shapes=[
            pltpu.VMEM((NY, TOK, WIDTH), BF),
            pltpu.VMEM((NX, NZ, NC, 4, SHARD, WIDTH), BF),
            pltpu.VMEM((2, TOK, WIDTH), F32),
            pltpu.VMEM((TOK, WIDTH), F32),
            pltpu.VMEM((2, TOK, 2 * DH), BF),
            pltpu.VMEM((2, TOK, MF), BF),
            pltpu.VMEM((2, TOK, MF), BF),
            pltpu.VMEM((2, MF, DH), F32),
            pltpu.VMEM((2, MF, 3 * DH), BF),
            pltpu.VMEM((2, TOK, 2 * DH), F32),
            pltpu.VMEM((2, SROWS, MF), F32),
            pltpu.VMEM((SROWS, MF), BF),
            pltpu.VMEM((SROWS, MF), BF),
            pltpu.VMEM((NZ, SLICE, MF), BF),
            pltpu.VMEM((NZ, SLICE, MF), BF),
            pltpu.VMEM((SLICE, MF), BF),
            pltpu.VMEM((NZ, SLICE, MF), BF),
            pltpu.VMEM((NZ, SLICE, MF), F32),
            pltpu.VMEM((NX, SLICE, MF), BF),
            pltpu.VMEM((NX, SLICE, MF), BF),
            pltpu.VMEM((NZ, SLICE, MF), BF),
            pltpu.VMEM((NZ, SLICE, MF), BF),
            pltpu.VMEM((SLICE, MF), F32),
            pltpu.VMEM((SROWS, MF), BF),
            pltpu.VMEM((SROWS, MF), BF),
            pltpu.VMEM((SROWS, MF), F32),
            pltpu.VMEM((TOK, 2 * DH), BF),
            pltpu.VMEM((2, 4, PIECES, PIECE, WIDTH), BF),
            pltpu.VMEM((2, 4, PIECES, PIECE, WIDTH), BF),
            pltpu.VMEM((TOK, WIDTH), BF),
            dma((6,)),
            dma((SENDS,)),
            dma((2, 4, PIECES)),
            dma((3, NZ)),
            dma((3, 6)),
            dma((3, 7)),
            dma((NZ,)),
            dma((NZ,)),
            dma((NX,)),
            dma((NX,)),
            dma((NZ,)),
            dma((2,)),
            dma((2, 4, PIECES)),
        ],
        compiler_params=pltpu.CompilerParams(
            collective_id=0, has_side_effects=True, vmem_limit_bytes=56 * 1024 * 1024
        ),
    )(tokens, w_query, w_key, w_value, features, w_out.T)


def solution(mesh):
    return jax.shard_map(
        body,
        mesh=mesh,
        in_specs=(
            P("ctx", "tp"),
            P("ctx", "tp"),
            P("ctx", "tp"),
            P("ctx", "tp"),
            P("tp", None, None),
            P("tp", "ctx"),
        ),
        out_specs=P("ctx", "tp"),
        check_vma=False,
    )
```

```python
import jax
import jax.numpy as jnp
from jax import lax
from jax.experimental import pallas as pl
from jax.experimental.pallas import tpu as pltpu
from jax.sharding import PartitionSpec as P

NX, NZ, NC, NY = 4, 8, 2, 8
GROUP = NZ * NC
TOK = 512
HALF = 256
PIECES = 4
PIECE = 128
WIDTH = 256
DH = 128
MF = 256
SHARD = 32
SLICE = 16
SROWS = DH + SLICE
SENDS = 192
BF = jnp.bfloat16
F32 = jnp.float32
NT = (((1,), (1,)), ((), ()))
TN = (((0,), (0,)), ((), ()))


def kernel(
    tok_ref, wq_ref, wk_ref, wv_ref, feat_ref, wo_ref, out_ref,
    tok, w, kv, q, vaug, phik, phiq, feat, fcat, nd, sacc, ssend, srecv, tsend, arecv, nsend, nrecv,
    excl, tot, ntot, psend, pfx, npre, fsend, frecv, own, attn, rs_send, rs_recv, result,
    loc_sem, ssem, tok_sem, z_sem, x_sem, sib_sem, a_sem, an_sem, b_sem, bn_sem, c_sem, j_sem, rs_sem,
):
    ctx = lax.axis_index("ctx")
    y = lax.axis_index("tp")
    c = lax.rem(ctx, NC)
    z = lax.rem(lax.div(ctx, NC), NZ)
    x = lax.div(ctx, GROUP)

    def at(xx, zz, cc):
        return {"ctx": (xx * NZ + zz) * NC + cc, "tp": y}

    def at_y(yy):
        return {"ctx": ctx, "tp": yy}

    def turn(v, by, n):
        return lax.rem(v + (by % n), n)

    ups = [at_y(turn(y, 1, NY)), at_y(turn(y, -1, NY))]
    sides = [at(turn(x, 1, NX), z, c), at(turn(x, -1, NX), z, c)]
    sib = at(x, z, 1 - c)

    barrier = pltpu.get_barrier_semaphore()
    greeted = (
        ups
        + [at(x, turn(z, d, NZ), c) for d in (4, 3, 5, 2, 6, 1, 7)]
        + [at(turn(x, d, NX), z, c) for d in (2, 1, 3)]
        + [sib]
    )
    for p in greeted:
        pl.semaphore_signal(barrier, inc=1, device_id=p, device_id_type=pl.DeviceIdType.MESH)

    loads = [
        pltpu.make_async_copy(src, dst, loc_sem.at[i])
        for i, (src, dst) in enumerate([
            (tok_ref, tok.at[y]),
            (wk_ref, w.at[x, z, c, 0]),
            (wv_ref, w.at[x, z, c, 1]),
            (wq_ref, w.at[x, z, c, 2]),
            (wo_ref, w.at[x, z, c, 3]),
            (feat_ref, feat),
        ])
    ]
    for copy in loads:
        copy.start()
    pl.semaphore_wait(barrier, len(greeted))

    sends = []

    def send(src, dst, rsem, dev):
        copy = pltpu.make_async_remote_copy(
            src_ref=src, dst_ref=dst, send_sem=ssem.at[len(sends)], recv_sem=rsem,
            device_id=dev, device_id_type=pl.DeviceIdType.MESH,
        )
        copy.start()
        sends.append(copy)

    def recv(dst, rsem):
        pltpu.make_async_copy(dst, dst, rsem).wait()

    def tok_owner(d, step):
        return turn(y, -step if d == 0 else step, NY)

    def tok_part(owner, r):
        return tok.at[owner, pl.ds(r * PIECE, PIECE)]

    def tok_send(d, step, r):
        part = tok_part(tok_owner(d, step), r)
        src = tok_ref.at[pl.ds(r * PIECE, PIECE)] if step == 0 else part
        send(src, part, tok_sem.at[d, step, r], ups[d])

    def tok_recv(d, step, r):
        recv(tok_part(tok_owner(d, step + 1), r), tok_sem.at[d, step, r])

    spans = (pl.ds(0, 2), pl.ds(2, 1), pl.ds(3, 1))

    def w_part(xx, zs, cc, part):
        return w.at[xx, zs, cc, spans[part]]

    def z_send(part):
        mine = w_part(x, z, c, part)
        for d in (4, 3, 5, 2, 6, 1, 7):
            send(mine, mine, z_sem.at[part, z], at(x, turn(z, d, NZ), c))

    def z_recv(part):
        for d in (1, 7, 2, 6, 3, 5, 4):
            zz = turn(z, d, NZ)
            recv(w_part(x, zz, c, part), z_sem.at[part, zz])

    every = pl.ds(0, NZ)
    halves = (pl.ds(0, NZ // 2), pl.ds(NZ // 2, NZ // 2))

    def sib_send(part, i, xx, zs):
        block = w_part(xx, zs, c, part)
        send(block, block, sib_sem.at[part, i], sib)

    def x_start(part):
        for i in range(2):
            for d in range(2):
                half = w_part(x, halves[d if i == 0 else 1 - d], c, part)
                send(half, half, x_sem.at[part, 2 * d + i], sides[d])
        sib_send(part, 0, x, every)

    def x_near(part, i):
        for d in range(2):
            xx = turn(x, -1 if d == 0 else 1, NX)
            zs = halves[d if i == 0 else 1 - d]
            half = w_part(xx, zs, c, part)
            recv(half, x_sem.at[part, 2 * d + i])
            if i == 0:
                send(half, half, x_sem.at[part, 4 + d], sides[d])
            sib_send(part, 1 + 2 * d + i, xx, zs)

    def x_far(part):
        xx = turn(x, 2, NX)
        for d in range(2):
            recv(w_part(xx, halves[d], c, part), x_sem.at[part, 4 + d])
            sib_send(part, 5 + d, xx, halves[d])

    def sib_recv(part):
        o = 1 - c
        recv(w_part(x, every, o, part), sib_sem.at[part, 0])
        for d in range(2):
            for i in range(2):
                xx = turn(x, -1 if d == 0 else 1, NX)
                recv(w_part(xx, halves[d if i == 0 else 1 - d], o, part), sib_sem.at[part, 1 + 2 * d + i])
            recv(w_part(turn(x, 2, NX), halves[d], o, part), sib_sem.at[part, 5 + d])

    for r in range(PIECES):
        for d in range(2):
            tok_send(d, 0, r)
    for copy in loads:
        copy.wait()
    z_send(0)

    for h in range(2):
        f = feat[h]
        hi = f.astype(BF)
        lo = (f - hi.astype(F32)).astype(BF)
        fcat[h] = jnp.concatenate([hi, hi, lo], axis=1)
        vaug[h, :, pl.ds(DH, DH)] = jnp.ones((TOK, DH), BF)

    def tok_pass(step, r):
        for d in range(2):
            tok_recv(d, step, r)
            tok_send(d, step + 1, r)

    for r in range(PIECES):
        tok_pass(0, r)
    z_recv(0)
    x_start(0)
    z_send(1)
    z_send(2)
    for r in range(PIECES):
        tok_pass(1, r)
    x_near(0, 0)
    for r in range(2):
        tok_recv(0, 2, r)
        tok_send(0, 3, r)
    x_near(0, 1)
    z_recv(1)
    x_start(1)
    for r in range(2, 4):
        tok_recv(1, 2, r)
        tok_send(1, 3, r)
    x_far(0)
    z_recv(2)
    sib_recv(0)

    def w_rows(s, k):
        return w[lax.div(s, 2), pl.ds(lax.rem(s, 2) * 4, 4), :, k].reshape(WIDTH, WIDTH)

    for r in range(2):
        tok_recv(0, 2, 2 + r)
        tok_recv(1, 2, r)

    early = [turn(y, d, NY) for d in (0, 1, -1, 2, -2, 3, -3)]

    @pl.loop(0, 2)
    def _(r):
        rows_r = pl.ds(pl.multiple_of(r * HALF, HALF), HALF)
        t = jnp.concatenate([tok[s, rows_r] for s in early], axis=1)
        for k in range(2):
            wide = jnp.concatenate([w_rows(s, k) for s in early], axis=0)
            kv[k, rows_r] = jnp.dot(t, wide, preferred_element_type=F32)


    def positive(p, h):
        s = p * (DH ** -0.25)
        half_square = 0.5 * jnp.sum(s * s, axis=-1, keepdims=True)
        hi = s.astype(BF)
        lo = (s - hi.astype(F32)).astype(BF)
        logits = lax.dot_general(
            jnp.concatenate([hi, lo, hi], axis=1), fcat[h], NT, preferred_element_type=F32
        )
        return jnp.exp(logits - half_square).astype(BF)

    last = turn(y, 4, NY)

    def key_pair(p):
        tok_recv(0, 3, p)
        tok_recv(1, 3, 2 + p)
        rows_p = [pl.ds(r * PIECE, PIECE) for r in (p, 2 + p)]
        t = jnp.concatenate([tok[last, rows_r] for rows_r in rows_p], axis=0)
        both = []
        for k in range(2):
            had = jnp.concatenate([kv[k, rows_r] for rows_r in rows_p], axis=0)
            both.append(had + jnp.dot(t, w_rows(last, k), preferred_element_type=F32))
        for h in range(2):
            head = slice(h * DH, (h + 1) * DH)
            maps = positive(both[0][:, head], h)
            vals = both[1][:, head].astype(BF)
            for i, rows_r in enumerate(rows_p):
                phik[h, rows_r] = maps[i * PIECE : (i + 1) * PIECE]
                vaug[h, rows_r, pl.ds(0, DH)] = vals[i * PIECE : (i + 1) * PIECE]

    def key_sums(h, p):
        spans_p = [pl.ds(r * PIECE, PIECE) for r in (p, 2 + p)]
        return lax.dot_general(
            jnp.concatenate([vaug[h, rows_r] for rows_r in spans_p], axis=0),
            jnp.concatenate([phik[h, rows_r] for rows_r in spans_p], axis=0),
            TN, preferred_element_type=F32,
        )[:SROWS]

    key_pair(0)
    for h in range(2):
        sacc[h] = key_sums(h, 0)
    key_pair(1)
    ssend[...] = (sacc[1 - c] + key_sums(1 - c, 1)).astype(BF)
    send(ssend, srecv, j_sem.at[0], sib)
    x_near(1, 0)
    own[...] = (sacc[c] + key_sums(c, 1)).astype(BF).astype(F32)
    recv(srecv, j_sem.at[0])
    chip = (own[...] + srecv[...].astype(F32)).astype(BF)
    tsend[...] = chip[:DH].reshape(NZ, SLICE, MF)
    nsend[...] = chip[DH:]

    for d in (4, 3, 5, 2, 6, 1, 7):
        zz = turn(z, d, NZ)
        send(tsend.at[zz], arecv.at[z], a_sem.at[z], at(x, zz, c))
    for d in (4, 3, 5, 2, 6, 1, 7):
        zz = turn(z, d, NZ)
        send(nsend, nrecv.at[z], an_sem.at[z], at(x, zz, c))
    arecv[z] = tsend[z]
    nrecv[z] = nsend[...]

    x_near(1, 1)
    x_start(2)
    x_far(1)
    sib_recv(1)

    @pl.loop(0, 2)
    def _(r):
        rows_r = pl.ds(pl.multiple_of(r * HALF, HALF), HALF)
        t = jnp.concatenate([tok[s, rows_r] for s in range(NY)], axis=1)
        q[rows_r] = jnp.dot(
            t, w[:, :, :, 2].reshape(NY * WIDTH, WIDTH), preferred_element_type=F32
        )

    for d in (1, 7, 2, 6, 3, 5, 4):
        zz = turn(z, d, NZ)
        recv(arecv.at[zz], a_sem.at[zz])
    run = jnp.zeros((SLICE, MF), F32)
    for i in range(NZ):
        excl[i] = run
        run = run + arecv[i].astype(F32)
    tot[x] = run.astype(BF)
    for d in (2, 1, 3):
        send(tot.at[x], tot.at[x], b_sem.at[x], at(turn(x, d, NX), z, c))

    for d in (1, 7, 2, 6, 3, 5, 4):
        zz = turn(z, d, NZ)
        recv(nrecv.at[zz], an_sem.at[zz])
    run = jnp.zeros((SLICE, MF), F32)
    for i in range(NZ):
        run = run + nrecv[i].astype(F32)
    ntot[x] = run.astype(BF)
    for d in (2, 1, 3):
        send(ntot.at[x], ntot.at[x], bn_sem.at[x], at(turn(x, d, NX), z, c))

    def local(h):
        for r in range(2):
            rows_r = pl.ds(r * HALF, HALF)
            upto = (r + 1) * HALF
            sc = lax.dot_general(
                phiq[h, rows_r], phik[h, pl.ds(0, upto)], NT, preferred_element_type=F32
            )
            row = lax.broadcasted_iota(jnp.int32, (HALF, upto), 0) + r * HALF
            col = lax.broadcasted_iota(jnp.int32, (HALF, upto), 1)
            sc = jnp.where(col <= row, sc, 0.0).astype(BF)
            nd[h, rows_r] = jnp.dot(sc, vaug[h, pl.ds(0, upto)], preferred_element_type=F32)

    x_near(2, 0)
    for h in range(2):
        phiq[h] = positive(q[:, pl.ds(h * DH, DH)], h)
    local(0)

    for d in range(1, NX):
        xx = turn(x, d, NX)
        recv(tot.at[xx], b_sem.at[xx])
    base = jnp.zeros((SLICE, MF), F32)
    for i in range(NX):
        base = base + jnp.where(i < x, tot[i].astype(F32), 0.0)
    for i in range(NZ):
        psend[i] = (excl[i] + base).astype(BF)
    for d in (4, 3, 5, 2, 6, 1, 7):
        zz = turn(z, d, NZ)
        send(psend.at[zz], pfx.at[z], c_sem.at[z], at(x, zz, c))
    pfx[z] = psend[z]

    x_near(2, 1)
    local(1)
    x_far(2)
    sib_recv(2)

    for d in range(1, NX):
        xx = turn(x, d, NX)
        recv(ntot.at[xx], bn_sem.at[xx])
    base = jnp.zeros((SLICE, MF), F32)
    for i in range(NX):
        base = base + jnp.where(i < x, ntot[i].astype(F32), 0.0)
    for i in range(NZ):
        base = base + jnp.where(i < z, nrecv[i].astype(F32), 0.0)
    npre[...] = base

    for d in (1, 7, 2, 6, 3, 5, 4):
        zz = turn(z, d, NZ)
        recv(pfx.at[zz], c_sem.at[zz])

    before = jnp.concatenate([pfx[...].reshape(DH, MF).astype(F32), npre[...]], axis=0)
    fsend[...] = (before + jnp.where(c == 0, own[...], 0.0)).astype(BF)
    send(fsend, frecv, j_sem.at[1], sib)
    state = (before + jnp.where(c == 0, 0.0, srecv[...].astype(F32))).astype(BF)

    def spread(sums):
        return jnp.concatenate([sums[:DH]] + [sums[DH:]] * (DH // SLICE), axis=0)

    def finish(h, state, r):
        rows_r = pl.ds(r * HALF, HALF)
        full = nd[h, rows_r] + lax.dot_general(
            phiq[h, rows_r], state, NT, preferred_element_type=F32
        )
        head = pl.ds(pl.multiple_of(h * DH, DH), DH)
        attn[rows_r, head] = (full[:, :DH] / full[:, DH:]).astype(BF)

    def share(dest, r):
        return lax.dot_general(
            attn[pl.ds(r * PIECE, PIECE)], w_rows(dest, 3), NT, preferred_element_type=F32
        )

    def rs_item(d, step, r, first):
        dest = turn(y, (4 - step) if d == 0 else (step - 4), NY)
        value = share(dest, r)
        if not first:
            recv(rs_recv.at[d, step - 1, r], rs_sem.at[d, step - 1, r])
            value = value + rs_recv[d, step - 1, r].astype(F32)
        rs_send[d, step, r] = value.astype(BF)
        send(rs_send.at[d, step, r], rs_recv.at[d, step, r], rs_sem.at[d, step, r], ups[d])

    before_ring = len(sends)
    waited = []

    def drain(count, stop):
        for copy in sends[len(waited) : min(len(waited) + count, stop)]:
            copy.wait_send()
            waited.append(copy)

    state = spread(state)
    finish(c, state, 0)
    finish(c, state, 1)
    recv(frecv, j_sem.at[1])
    state = spread(frecv[...])
    finish(1 - c, state, 0)
    for r in range(2):
        rs_item(0, 0, r, True)
    finish(1 - c, state, 1)
    for r in range(2):
        rs_item(1, 0, 2 + r, True)
    for step in range(1, 4):
        for k in range(4):
            for d in range(2):
                rs_item(d, step, (k + 2 * (1 - d)) % 4, step == 1 and k < 2)
                drain(before_ring // 20, before_ring)
    drain(len(sends), len(sends) - 8)
    stores = []
    for r in range(PIECES):
        value = share(y, r)
        for d in range(2):
            recv(rs_recv.at[d, 3, r], rs_sem.at[d, 3, r])
            value = value + rs_recv[d, 3, r].astype(F32)
        rows_r = pl.ds(r * PIECE, PIECE)
        result[rows_r] = value.astype(BF)
        store = pltpu.make_async_copy(result.at[rows_r], out_ref.at[rows_r], loc_sem.at[r])
        store.start()
        stores.append(store)

    drain(len(sends), len(sends))
    for store in stores:
        store.wait()


def body(tokens, w_query, w_key, w_value, features, w_out):
    hbm = pl.BlockSpec(memory_space=pl.ANY)
    dma = pltpu.SemaphoreType.DMA
    return pl.pallas_call(
        kernel,
        out_shape=jax.ShapeDtypeStruct((TOK, WIDTH), BF),
        in_specs=[hbm] * 6,
        out_specs=hbm,
        scratch_shapes=[
            pltpu.VMEM((NY, TOK, WIDTH), BF),
            pltpu.VMEM((NX, NZ, NC, 4, SHARD, WIDTH), BF),
            pltpu.VMEM((2, TOK, WIDTH), F32),
            pltpu.VMEM((TOK, WIDTH), F32),
            pltpu.VMEM((2, TOK, 2 * DH), BF),
            pltpu.VMEM((2, TOK, MF), BF),
            pltpu.VMEM((2, TOK, MF), BF),
            pltpu.VMEM((2, MF, DH), F32),
            pltpu.VMEM((2, MF, 3 * DH), BF),
            pltpu.VMEM((2, TOK, 2 * DH), F32),
            pltpu.VMEM((2, SROWS, MF), F32),
            pltpu.VMEM((SROWS, MF), BF),
            pltpu.VMEM((SROWS, MF), BF),
            pltpu.VMEM((NZ, SLICE, MF), BF),
            pltpu.VMEM((NZ, SLICE, MF), BF),
            pltpu.VMEM((SLICE, MF), BF),
            pltpu.VMEM((NZ, SLICE, MF), BF),
            pltpu.VMEM((NZ, SLICE, MF), F32),
            pltpu.VMEM((NX, SLICE, MF), BF),
            pltpu.VMEM((NX, SLICE, MF), BF),
            pltpu.VMEM((NZ, SLICE, MF), BF),
            pltpu.VMEM((NZ, SLICE, MF), BF),
            pltpu.VMEM((SLICE, MF), F32),
            pltpu.VMEM((SROWS, MF), BF),
            pltpu.VMEM((SROWS, MF), BF),
            pltpu.VMEM((SROWS, MF), F32),
            pltpu.VMEM((TOK, 2 * DH), BF),
            pltpu.VMEM((2, 4, PIECES, PIECE, WIDTH), BF),
            pltpu.VMEM((2, 4, PIECES, PIECE, WIDTH), BF),
            pltpu.VMEM((TOK, WIDTH), BF),
            dma((6,)),
            dma((SENDS,)),
            dma((2, 4, PIECES)),
            dma((3, NZ)),
            dma((3, 6)),
            dma((3, 7)),
            dma((NZ,)),
            dma((NZ,)),
            dma((NX,)),
            dma((NX,)),
            dma((NZ,)),
            dma((2,)),
            dma((2, 4, PIECES)),
        ],
        compiler_params=pltpu.CompilerParams(
            collective_id=0, has_side_effects=True, vmem_limit_bytes=56 * 1024 * 1024
        ),
    )(tokens, w_query, w_key, w_value, features, w_out.T)


def solution(mesh):
    return jax.shard_map(
        body,
        mesh=mesh,
        in_specs=(
            P("ctx", "tp"),
            P("ctx", "tp"),
            P("ctx", "tp"),
            P("ctx", "tp"),
            P("tp", None, None),
            P("tp", "ctx"),
        ),
        out_specs=P("ctx", "tp"),
        check_vma=False,
    )
```

```python
import jax
import jax.numpy as jnp
from jax import lax
from jax.experimental import pallas as pl
from jax.experimental.pallas import tpu as pltpu
from jax.sharding import PartitionSpec as P

NX, NZ, NC, NY = 4, 8, 2, 8
GROUP = NZ * NC
TOK = 512
HALF = 256
PIECES = 4
PIECE = 128
WIDTH = 256
DH = 128
MF = 256
SHARD = 32
SLICE = 16
SROWS = DH + SLICE
SENDS = 192
BF = jnp.bfloat16
F32 = jnp.float32
NT = (((1,), (1,)), ((), ()))
TN = (((0,), (0,)), ((), ()))


def kernel(
    tok_ref, wq_ref, wk_ref, wv_ref, feat_ref, wo_ref, out_ref,
    tok, w, kv, q, vaug, phik, phiq, feat, fcat, nd, sacc, ssend, srecv, tsend, arecv, nsend, nrecv,
    excl, tot, ntot, psend, pfx, npre, fsend, frecv, own, attn, rs_send, rs_recv, result, wout,
    loc_sem, ssem, tok_sem, z_sem, x_sem, sib_sem, a_sem, an_sem, b_sem, bn_sem, c_sem, j_sem, rs_sem,
):
    ctx = lax.axis_index("ctx")
    y = lax.axis_index("tp")
    c = lax.rem(ctx, NC)
    z = lax.rem(lax.div(ctx, NC), NZ)
    x = lax.div(ctx, GROUP)

    def at(xx, zz, cc):
        return {"ctx": (xx * NZ + zz) * NC + cc, "tp": y}

    def at_y(yy):
        return {"ctx": ctx, "tp": yy}

    def turn(v, by, n):
        return lax.rem(v + (by % n), n)

    ups = [at_y(turn(y, 1, NY)), at_y(turn(y, -1, NY))]
    sides = [at(turn(x, 1, NX), z, c), at(turn(x, -1, NX), z, c)]
    sib = at(x, z, 1 - c)

    barrier = pltpu.get_barrier_semaphore()
    greeted = (
        ups
        + [at(x, turn(z, d, NZ), c) for d in (4, 3, 5, 2, 6, 1, 7)]
        + [at(turn(x, d, NX), z, c) for d in (2, 1, 3)]
        + [sib]
    )
    for p in greeted:
        pl.semaphore_signal(barrier, inc=1, device_id=p, device_id_type=pl.DeviceIdType.MESH)

    loads = [
        pltpu.make_async_copy(src, dst, loc_sem.at[i])
        for i, (src, dst) in enumerate([
            (tok_ref, tok.at[y]),
            (wk_ref, w.at[x, z, c, 0]),
            (wv_ref, w.at[x, z, c, 1]),
            (wq_ref, w.at[x, z, c, 2]),
            (wo_ref, w.at[x, z, c, 3]),
            (feat_ref, feat),
        ])
    ]
    for copy in loads[1:]:
        copy.start()
    for copy in loads[1:]:
        copy.wait()
    pl.semaphore_wait(barrier, len(greeted))

    sends = []

    def send(src, dst, rsem, dev):
        copy = pltpu.make_async_remote_copy(
            src_ref=src, dst_ref=dst, send_sem=ssem.at[len(sends)], recv_sem=rsem,
            device_id=dev, device_id_type=pl.DeviceIdType.MESH,
        )
        copy.start()
        sends.append(copy)

    def recv(dst, rsem):
        pltpu.make_async_copy(dst, dst, rsem).wait()

    def tok_owner(d, step):
        return turn(y, -step if d == 0 else step, NY)

    def tok_part(owner, r):
        return tok.at[owner, pl.ds(r * PIECE, PIECE)]

    def tok_send(d, step, r):
        part = tok_part(tok_owner(d, step), r)
        src = tok_ref.at[pl.ds(r * PIECE, PIECE)] if step == 0 else part
        send(src, part, tok_sem.at[d, step, r], ups[d])

    def tok_recv(d, step, r):
        recv(tok_part(tok_owner(d, step + 1), r), tok_sem.at[d, step, r])

    spans = (pl.ds(0, 2), pl.ds(2, 1), pl.ds(3, 1))

    def w_part(xx, zs, cc, part):
        return w.at[xx, zs, cc, spans[part]]

    def z_send(part):
        mine = w_part(x, z, c, part)
        for d in (4, 3, 5, 2, 6, 1, 7):
            send(mine, mine, z_sem.at[part, z], at(x, turn(z, d, NZ), c))

    def z_recv(part):
        for d in (1, 7, 2, 6, 3, 5, 4):
            zz = turn(z, d, NZ)
            recv(w_part(x, zz, c, part), z_sem.at[part, zz])

    every = pl.ds(0, NZ)
    halves = (pl.ds(0, NZ // 2), pl.ds(NZ // 2, NZ // 2))

    def sib_send(part, i, xx, zs):
        block = w_part(xx, zs, c, part)
        send(block, block, sib_sem.at[part, i], sib)

    def x_start(part):
        for i in range(2):
            for d in range(2):
                half = w_part(x, halves[d if i == 0 else 1 - d], c, part)
                send(half, half, x_sem.at[part, 2 * d + i], sides[d])
        sib_send(part, 0, x, every)

    def x_near(part, i):
        for d in range(2):
            xx = turn(x, -1 if d == 0 else 1, NX)
            zs = halves[d if i == 0 else 1 - d]
            half = w_part(xx, zs, c, part)
            recv(half, x_sem.at[part, 2 * d + i])
            if i == 0:
                send(half, half, x_sem.at[part, 4 + d], sides[d])
            sib_send(part, 1 + 2 * d + i, xx, zs)

    def x_far(part):
        xx = turn(x, 2, NX)
        for d in range(2):
            recv(w_part(xx, halves[d], c, part), x_sem.at[part, 4 + d])
            sib_send(part, 5 + d, xx, halves[d])

    def sib_recv(part):
        o = 1 - c
        recv(w_part(x, every, o, part), sib_sem.at[part, 0])
        for d in range(2):
            for i in range(2):
                xx = turn(x, -1 if d == 0 else 1, NX)
                recv(w_part(xx, halves[d if i == 0 else 1 - d], o, part), sib_sem.at[part, 1 + 2 * d + i])
            recv(w_part(turn(x, 2, NX), halves[d], o, part), sib_sem.at[part, 5 + d])

    for r in range(PIECES):
        for d in range(2):
            tok_send(d, 0, r)
    loads[0].start()
    z_send(0)
    loads[0].wait()

    for h in range(2):
        f = feat[h]
        hi = f.astype(BF)
        lo = (f - hi.astype(F32)).astype(BF)
        fcat[h] = jnp.concatenate([hi, hi, lo], axis=1)
        vaug[h, :, pl.ds(DH, DH)] = jnp.ones((TOK, DH), BF)

    def tok_pass(step, r):
        for d in range(2):
            tok_recv(d, step, r)
            tok_send(d, step + 1, r)

    for r in range(PIECES):
        tok_pass(0, r)
    z_recv(0)
    x_start(0)
    z_send(1)
    z_send(2)
    for r in range(PIECES):
        tok_pass(1, r)
    x_near(0, 0)
    for r in range(2):
        tok_recv(0, 2, r)
        tok_send(0, 3, r)
    x_near(0, 1)
    z_recv(1)
    x_start(1)
    for r in range(2, 4):
        tok_recv(1, 2, r)
        tok_send(1, 3, r)
    x_far(0)
    z_recv(2)
    sib_recv(0)

    def w_rows(s, k):
        return w[lax.div(s, 2), pl.ds(lax.rem(s, 2) * 4, 4), :, k].reshape(WIDTH, WIDTH)

    for r in range(2):
        tok_recv(0, 2, 2 + r)
        tok_recv(1, 2, r)

    early = [turn(y, d, NY) for d in (0, 1, -1, 2, -2, 3, -3)]

    @pl.loop(0, 2)
    def _(r):
        rows_r = pl.ds(pl.multiple_of(r * HALF, HALF), HALF)
        t = jnp.concatenate([tok[s, rows_r] for s in early], axis=1)
        for k in range(2):
            wide = jnp.concatenate([w_rows(s, k) for s in early], axis=0)
            kv[k, rows_r] = jnp.dot(t, wide, preferred_element_type=F32)


    def positive(p, h):
        s = p * (DH ** -0.25)
        half_square = 0.5 * jnp.sum(s * s, axis=-1, keepdims=True)
        hi = s.astype(BF)
        lo = (s - hi.astype(F32)).astype(BF)
        logits = lax.dot_general(
            jnp.concatenate([hi, lo, hi], axis=1), fcat[h], NT, preferred_element_type=F32
        )
        return jnp.exp(logits - half_square).astype(BF)

    last = turn(y, 4, NY)

    def key_pair(p):
        tok_recv(0, 3, p)
        tok_recv(1, 3, 2 + p)
        rows_p = [pl.ds(r * PIECE, PIECE) for r in (p, 2 + p)]
        t = jnp.concatenate([tok[last, rows_r] for rows_r in rows_p], axis=0)
        both = []
        for k in range(2):
            had = jnp.concatenate([kv[k, rows_r] for rows_r in rows_p], axis=0)
            both.append(had + jnp.dot(t, w_rows(last, k), preferred_element_type=F32))
        for h in range(2):
            head = slice(h * DH, (h + 1) * DH)
            maps = positive(both[0][:, head], h)
            vals = both[1][:, head].astype(BF)
            for i, rows_r in enumerate(rows_p):
                phik[h, rows_r] = maps[i * PIECE : (i + 1) * PIECE]
                vaug[h, rows_r, pl.ds(0, DH)] = vals[i * PIECE : (i + 1) * PIECE]

    def key_sums(h, p):
        spans_p = [pl.ds(r * PIECE, PIECE) for r in (p, 2 + p)]
        return lax.dot_general(
            jnp.concatenate([vaug[h, rows_r] for rows_r in spans_p], axis=0),
            jnp.concatenate([phik[h, rows_r] for rows_r in spans_p], axis=0),
            TN, preferred_element_type=F32,
        )[:SROWS]

    key_pair(0)
    for h in range(2):
        sacc[h] = key_sums(h, 0)
    key_pair(1)
    ssend[...] = (sacc[1 - c] + key_sums(1 - c, 1)).astype(BF)
    send(ssend, srecv, j_sem.at[0], sib)
    x_near(1, 0)
    own[...] = (sacc[c] + key_sums(c, 1)).astype(BF).astype(F32)
    recv(srecv, j_sem.at[0])
    chip = (own[...] + srecv[...].astype(F32)).astype(BF)
    tsend[...] = chip[:DH].reshape(NZ, SLICE, MF)
    nsend[...] = chip[DH:]

    for d in (4, 3, 5, 2, 6, 1, 7):
        zz = turn(z, d, NZ)
        send(tsend.at[zz], arecv.at[z], a_sem.at[z], at(x, zz, c))
    for d in (4, 3, 5, 2, 6, 1, 7):
        zz = turn(z, d, NZ)
        send(nsend, nrecv.at[z], an_sem.at[z], at(x, zz, c))
    arecv[z] = tsend[z]
    nrecv[z] = nsend[...]

    x_near(1, 1)
    x_start(2)
    x_far(1)
    sib_recv(1)

    @pl.loop(0, 2)
    def _(r):
        rows_r = pl.ds(pl.multiple_of(r * HALF, HALF), HALF)
        t = jnp.concatenate([tok[s, rows_r] for s in range(NY)], axis=1)
        q[rows_r] = jnp.dot(
            t, w[:, :, :, 2].reshape(NY * WIDTH, WIDTH), preferred_element_type=F32
        )

    for d in (1, 7, 2, 6, 3, 5, 4):
        zz = turn(z, d, NZ)
        recv(arecv.at[zz], a_sem.at[zz])
    run = jnp.zeros((SLICE, MF), F32)
    for i in range(NZ):
        excl[i] = run
        run = run + arecv[i].astype(F32)
    tot[x] = run.astype(BF)
    for d in (2, 1, 3):
        send(tot.at[x], tot.at[x], b_sem.at[x], at(turn(x, d, NX), z, c))

    for d in (1, 7, 2, 6, 3, 5, 4):
        zz = turn(z, d, NZ)
        recv(nrecv.at[zz], an_sem.at[zz])
    run = jnp.zeros((SLICE, MF), F32)
    for i in range(NZ):
        run = run + nrecv[i].astype(F32)
    ntot[x] = run.astype(BF)
    for d in (2, 1, 3):
        send(ntot.at[x], ntot.at[x], bn_sem.at[x], at(turn(x, d, NX), z, c))

    def local(h):
        for r in range(2):
            rows_r = pl.ds(r * HALF, HALF)
            upto = (r + 1) * HALF
            sc = lax.dot_general(
                phiq[h, rows_r], phik[h, pl.ds(0, upto)], NT, preferred_element_type=F32
            )
            row = lax.broadcasted_iota(jnp.int32, (HALF, upto), 0) + r * HALF
            col = lax.broadcasted_iota(jnp.int32, (HALF, upto), 1)
            sc = jnp.where(col <= row, sc, 0.0).astype(BF)
            nd[h, rows_r] = jnp.dot(sc, vaug[h, pl.ds(0, upto)], preferred_element_type=F32)

    x_near(2, 0)
    for h in range(2):
        phiq[h] = positive(q[:, pl.ds(h * DH, DH)], h)
    local(0)

    for d in range(1, NX):
        xx = turn(x, d, NX)
        recv(tot.at[xx], b_sem.at[xx])
    base = jnp.zeros((SLICE, MF), F32)
    for i in range(NX):
        base = base + jnp.where(i < x, tot[i].astype(F32), 0.0)
    for i in range(NZ):
        psend[i] = (excl[i] + base).astype(BF)
    for d in (4, 3, 5, 2, 6, 1, 7):
        zz = turn(z, d, NZ)
        send(psend.at[zz], pfx.at[z], c_sem.at[z], at(x, zz, c))
    pfx[z] = psend[z]

    x_near(2, 1)
    local(1)
    x_far(2)
    sib_recv(2)

    @pl.loop(0, NY)
    def _(s):
        wout[s] = w_rows(s, 3).T


    for d in range(1, NX):
        xx = turn(x, d, NX)
        recv(ntot.at[xx], bn_sem.at[xx])
    base = jnp.zeros((SLICE, MF), F32)
    for i in range(NX):
        base = base + jnp.where(i < x, ntot[i].astype(F32), 0.0)
    for i in range(NZ):
        base = base + jnp.where(i < z, nrecv[i].astype(F32), 0.0)
    npre[...] = base

    for d in (1, 7, 2, 6, 3, 5, 4):
        zz = turn(z, d, NZ)
        recv(pfx.at[zz], c_sem.at[zz])

    before = jnp.concatenate([pfx[...].reshape(DH, MF).astype(F32), npre[...]], axis=0)
    fsend[...] = (before + jnp.where(c == 0, own[...], 0.0)).astype(BF)
    send(fsend, frecv, j_sem.at[1], sib)
    state = (before + jnp.where(c == 0, 0.0, srecv[...].astype(F32))).astype(BF)

    def spread(sums):
        return jnp.concatenate([sums[:DH]] + [sums[DH:]] * (DH // SLICE), axis=0)

    def finish(h, state, r):
        rows_r = pl.ds(r * HALF, HALF)
        full = nd[h, rows_r] + lax.dot_general(
            phiq[h, rows_r], state, NT, preferred_element_type=F32
        )
        head = pl.ds(pl.multiple_of(h * DH, DH), DH)
        attn[rows_r, head] = (full[:, :DH] / full[:, DH:]).astype(BF)

    def share(dest, r):
        return jnp.dot(attn[pl.ds(r * PIECE, PIECE)], wout[dest], preferred_element_type=F32)

    def rs_item(d, step, r, first):
        dest = turn(y, (4 - step) if d == 0 else (step - 4), NY)
        value = share(dest, r)
        if not first:
            recv(rs_recv.at[d, step - 1, r], rs_sem.at[d, step - 1, r])
            value = value + rs_recv[d, step - 1, r].astype(F32)
        rs_send[d, step, r] = value.astype(BF)
        send(rs_send.at[d, step, r], rs_recv.at[d, step, r], rs_sem.at[d, step, r], ups[d])

    before_ring = len(sends)
    waited = []

    def drain(count, stop):
        for copy in sends[len(waited) : min(len(waited) + count, stop)]:
            copy.wait_send()
            waited.append(copy)

    state = spread(state)
    finish(c, state, 0)
    finish(c, state, 1)
    recv(frecv, j_sem.at[1])
    state = spread(frecv[...])
    finish(1 - c, state, 0)
    for r in range(2):
        rs_item(0, 0, r, True)
    finish(1 - c, state, 1)
    for r in range(2):
        rs_item(1, 0, 2 + r, True)
    for step in range(1, 4):
        for k in range(4):
            for d in range(2):
                rs_item(d, step, (k + 2 * (1 - d)) % 4, step == 1 and k < 2)
                drain(before_ring // 20, before_ring)
    drain(len(sends), len(sends) - 8)
    stores = []
    for r in range(PIECES):
        value = share(y, r)
        for d in range(2):
            recv(rs_recv.at[d, 3, r], rs_sem.at[d, 3, r])
            value = value + rs_recv[d, 3, r].astype(F32)
        rows_r = pl.ds(r * PIECE, PIECE)
        result[rows_r] = value.astype(BF)
        store = pltpu.make_async_copy(result.at[rows_r], out_ref.at[rows_r], loc_sem.at[r])
        store.start()
        stores.append(store)

    drain(len(sends), len(sends))
    for store in stores:
        store.wait()


def body(tokens, w_query, w_key, w_value, features, w_out):
    hbm = pl.BlockSpec(memory_space=pl.ANY)
    dma = pltpu.SemaphoreType.DMA
    return pl.pallas_call(
        kernel,
        out_shape=jax.ShapeDtypeStruct((TOK, WIDTH), BF),
        in_specs=[hbm] * 6,
        out_specs=hbm,
        scratch_shapes=[
            pltpu.VMEM((NY, TOK, WIDTH), BF),
            pltpu.VMEM((NX, NZ, NC, 4, SHARD, WIDTH), BF),
            pltpu.VMEM((2, TOK, WIDTH), F32),
            pltpu.VMEM((TOK, WIDTH), F32),
            pltpu.VMEM((2, TOK, 2 * DH), BF),
            pltpu.VMEM((2, TOK, MF), BF),
            pltpu.VMEM((2, TOK, MF), BF),
            pltpu.VMEM((2, MF, DH), F32),
            pltpu.VMEM((2, MF, 3 * DH), BF),
            pltpu.VMEM((2, TOK, 2 * DH), F32),
            pltpu.VMEM((2, SROWS, MF), F32),
            pltpu.VMEM((SROWS, MF), BF),
            pltpu.VMEM((SROWS, MF), BF),
            pltpu.VMEM((NZ, SLICE, MF), BF),
            pltpu.VMEM((NZ, SLICE, MF), BF),
            pltpu.VMEM((SLICE, MF), BF),
            pltpu.VMEM((NZ, SLICE, MF), BF),
            pltpu.VMEM((NZ, SLICE, MF), F32),
            pltpu.VMEM((NX, SLICE, MF), BF),
            pltpu.VMEM((NX, SLICE, MF), BF),
            pltpu.VMEM((NZ, SLICE, MF), BF),
            pltpu.VMEM((NZ, SLICE, MF), BF),
            pltpu.VMEM((SLICE, MF), F32),
            pltpu.VMEM((SROWS, MF), BF),
            pltpu.VMEM((SROWS, MF), BF),
            pltpu.VMEM((SROWS, MF), F32),
            pltpu.VMEM((TOK, 2 * DH), BF),
            pltpu.VMEM((2, 4, PIECES, PIECE, WIDTH), BF),
            pltpu.VMEM((2, 4, PIECES, PIECE, WIDTH), BF),
            pltpu.VMEM((TOK, WIDTH), BF),
            pltpu.VMEM((NY, WIDTH, WIDTH), BF),
            dma((6,)),
            dma((SENDS,)),
            dma((2, 4, PIECES)),
            dma((3, NZ)),
            dma((3, 6)),
            dma((3, 7)),
            dma((NZ,)),
            dma((NZ,)),
            dma((NX,)),
            dma((NX,)),
            dma((NZ,)),
            dma((2,)),
            dma((2, 4, PIECES)),
        ],
        compiler_params=pltpu.CompilerParams(
            collective_id=0, has_side_effects=True, vmem_limit_bytes=56 * 1024 * 1024
        ),
    )(tokens, w_query, w_key, w_value, features, w_out.T)


def solution(mesh):
    return jax.shard_map(
        body,
        mesh=mesh,
        in_specs=(
            P("ctx", "tp"),
            P("ctx", "tp"),
            P("ctx", "tp"),
            P("ctx", "tp"),
            P("tp", None, None),
            P("tp", "ctx"),
        ),
        out_specs=P("ctx", "tp"),
        check_vma=False,
    )
```
